256 devices in a mesh: grp: 2 (over x_lo), tile: 128 (over z, y, x_hi, core).
Axes of the slice: x: 4 (x_hi: 2, x_lo: 2; x = x_hi * 2 + x_lo), y: 4, z: 8, core: 2. Of those that a mesh axis runs over, the one named last changes fastest.
Arguments:
- fine_probe: bfloat16 [64, 2621440], P(None, ('grp', 'tile')), may hold values from -6 to 6
- coarse_probe: bfloat16 [64, 8192], P(None, ('grp', 'tile')), may hold values from -6 to 6
- fine_diag: bfloat16 [2621440, 128], P(('grp', 'tile'))
- fine_cond: bfloat16 [2621440, 128], P(('grp', 'tile')), may hold values from -0.5 to 0.5
- fine_nbr: int32 [20480, 128], P(('grp', 'tile')), may hold values from -1 to 19327, as said below
- coarse_diag: bfloat16 [8192, 128], P(('grp', 'tile'))
- coarse_cond: bfloat16 [8192, 128], P(('grp', 'tile')), may hold values from -0.5 to 0.5
- coarse_nbr: int32 [64, 128], replicated, may hold values from -1 to 8063, as said below
Outputs:
- fine_out: bfloat16 [64, 2621440], P(None, ('grp', 'tile'))
- fine_back: float32 [64, 2621440], P(None, ('grp', 'tile'))
- coarse_out: bfloat16 [64, 8192], P(None, ('grp', 'tile'))
- coarse_back: float32 [64, 8192], P(None, ('grp', 'tile'))
The draws below stay inside these ranges and needn't reach their ends.
Inputs may be any that keep to these rules, and one draw needn't show every extreme that they name: `fine_nbr`: row b concerns fine block b, of device d = b // 80, whose points are fine points 128 b onward. Slots 0 to 63 name coarse points (values below 8192). The others are -1 for a padded slot, or a value 8192 + j with j < 1024 naming the fine point 80 * 128 d - 1024 + j (the last 1024 fine points of the device before it along tile within the same grp index; never for tile index 0), or a value 8192 + 1024 + j naming the fine point 80 * 128 d + j, an earlier point of the same device below 128 * b. `coarse_nbr`: row k lists coarse points of earlier coarse blocks (below 128 * k), or -1 for a padded slot.
All inputs are finite; a program needn't handle non-finite values.
Results may differ from the reference program's by a relative error of at most 0.0055.
Values may be sent and summed in bfloat16 or wider, within the bound.
A program may use at most 128 MiB of HBM per device.

```python
import math
import jax
import jax.numpy as jnp
from jax import lax

PROBES = 64
BLOCK = 128
NBRS = 128
FB = 80
COARSE_DEV = 32
RIM = 1024
TILES = 128
NC = 8192
NCB = 64
NFB = 20480
NF = 2621440


def triangle_rows(key, rows):
    key_diag, key_off = jax.random.split(key)
    row_pos = (jnp.arange(rows) % BLOCK)[:, None]
    col_pos = jnp.arange(BLOCK)[None, :]
    diag_vals = jnp.exp(jax.random.uniform(key_diag, (rows, 1), jnp.float32, 0.0, math.log(3.0)))
    off_vals = 0.08 * jax.random.normal(key_off, (rows, BLOCK), jnp.float32)
    values = jnp.where(col_pos == row_pos, diag_vals, jnp.where(col_pos < row_pos, off_vals, 0.0))
    return values.astype(jnp.bfloat16)


def draw_fine_diag(key, part):
    return triangle_rows(key, NF)


def draw_coarse_diag(key, part):
    return triangle_rows(key, NC)


def draw_fine_nbr(key, part):
    half_slots = NBRS // 2
    rest_slots = NBRS - half_slots
    groups = NC // (COARSE_DEV * TILES)
    block_ids = jnp.arange(NFB)[:, None]
    device_ids = block_ids // FB
    local_block = block_ids % FB
    tile_ids = device_ids % TILES
    key_coarse, key_pick, key_side, key_live = jax.random.split(key, 4)
    key_step, key_group, key_point = jax.random.split(key_coarse, 3)
    tile_step = jax.random.randint(key_step, (NFB, half_slots), -1, 2)
    owner_group = jax.random.randint(key_group, (NFB, half_slots), 0, groups)
    owner_point = jax.random.randint(key_point, (NFB, half_slots), 0, COARSE_DEV)
    owner_tile = (tile_ids + tile_step + TILES) % TILES
    coarse_part = (owner_group * TILES + owner_tile) * COARSE_DEV + owner_point
    picks = jax.random.randint(key_pick, (NFB, rest_slots), 0, 2 ** 30)
    sides = jax.random.randint(key_side, (NFB, rest_slots), 0, 2)
    have_rim = tile_ids > 0
    have_own = local_block > 0
    use_rim = jnp.where(have_rim & have_own, sides == 1, have_rim)
    rim_index = NC + picks % RIM
    own_index = NC + RIM + picks % jnp.maximum(local_block * BLOCK, 1)
    fine_part = jnp.where(use_rim, rim_index, own_index)
    live_count = jax.random.randint(key_live, (NFB, 1), 8, rest_slots + 1)
    slot_pos = jnp.arange(rest_slots)[None, :]
    keep = (slot_pos < live_count) & (have_rim | have_own)
    fine_part = jnp.where(keep, fine_part, -1)
    fine_part = fine_part.at[NFB - 1, 0].set(NC + RIM + (FB - 1) * BLOCK - 1)
    return jnp.concatenate([coarse_part, fine_part], axis=1).astype(jnp.int32)


def draw_coarse_nbr(key, part):
    block_ids = jnp.arange(NCB)[:, None]
    key_pick, key_live = jax.random.split(key)
    picks = jax.random.randint(key_pick, (NCB, NBRS), 0, 2 ** 30)
    chosen = picks % jnp.maximum(block_ids * BLOCK, 1)
    live_count = jax.random.randint(key_live, (NCB, 1), 16, NBRS + 1)
    slot_pos = jnp.arange(NBRS)[None, :]
    keep = (slot_pos < live_count) & (block_ids > 0)
    links = jnp.where(keep, chosen, -1)
    links = links.at[NCB - 1, 0].set(NC - BLOCK - 1)
    return links.astype(jnp.int32)


def block_levels(stream_key, shape, cuts, smallest, top_value):
    factor_of, own = 1.0, jax.random.fold_in(stream_key, 6)
    for axis_at, parts in cuts:
        draws = jnp.exp(jax.random.uniform(jax.random.fold_in(own, axis_at), (parts,), jnp.float32, smallest / len(cuts), top_value / len(cuts)))
        factor_of = factor_of * jnp.repeat(draws, shape[axis_at] // parts).reshape([-1 if axis == axis_at else 1 for axis in range(len(shape))])
    return factor_of


def noise(rng, shape, width, most, shards=(), kind=jnp.bfloat16):
    factor_of = block_levels(rng, shape, shards, -0.22, 0.18) if shards else 1.0
    values = jax.random.normal(rng, shape, jnp.float32) * width * factor_of
    return jnp.minimum(jnp.maximum(values, -most), most).astype(kind)


def setup_inputs(seed: int = 0) -> dict:
    key_list = jax.random.split(jax.random.key(seed), 9)
    return {
        "fine_probe": noise(key_list[0], (PROBES, NF), 1.0, 6.0, ((1, 256),)),
        "coarse_probe": noise(key_list[1], (PROBES, NC), 1.0, 6.0, ((1, 256),)),
        "fine_diag": draw_fine_diag(jax.random.fold_in(key_list[8], 71), 0),
        "fine_cond": noise(key_list[3], (NF, NBRS), NBRS ** -0.5, 0.5, ((0, 256),)),
        "fine_nbr": draw_fine_nbr(jax.random.fold_in(key_list[8], 71), 0),
        "coarse_diag": draw_coarse_diag(jax.random.fold_in(key_list[8], 71), 0),
        "coarse_cond": noise(key_list[6], (NC, NBRS), NBRS ** -0.5, 0.5, ((0, 256),)),
        "coarse_nbr": draw_coarse_nbr(jax.random.fold_in(key_list[8], 71), 0),
    }


def block_pass(own_probe, near_vals, block_diag, block_cond, valid):
    own_wide = own_probe.astype(jnp.float32)
    near_wide = near_vals.astype(jnp.float32)
    diag_wide = block_diag.astype(jnp.float32)
    cond_wide = block_cond.astype(jnp.float32)
    forward = jnp.einsum("pbq,bkq->pbk", own_wide, diag_wide) + jnp.einsum("pbs,bks->pbk", near_wide, cond_wide)
    result = lax.optimization_barrier(forward.astype(jnp.bfloat16))
    result_wide = result.astype(jnp.float32)
    back_own = jnp.einsum("pbk,bkq->pbq", result_wide, diag_wide)
    back_near = jnp.einsum("pbk,bks->pbs", result_wide, cond_wide)
    back_near = jnp.where(valid[None], back_near, jnp.zeros((), back_near.dtype))
    return result, back_own, back_near


def reference(fine_probe, coarse_probe, fine_diag, fine_cond, fine_nbr, coarse_diag, coarse_cond, coarse_nbr):
    probes = fine_probe.shape[0]
    coarse_pts = coarse_probe.shape[1]
    fine_pts = fine_probe.shape[1]
    block_len = fine_diag.shape[1]
    slot_count = fine_nbr.shape[1]
    coarse_blocks = coarse_nbr.shape[0]
    stretch_count = fine_nbr.shape[0] // FB
    probe_all = jnp.concatenate([coarse_probe, fine_probe], axis=1)

    owner_dev = (jnp.arange(fine_nbr.shape[0], dtype=jnp.int32) // FB)[:, None].astype(jnp.int32)
    shifted = (fine_nbr - RIM + owner_dev * (FB * block_len)).astype(jnp.int32)
    fine_global = jnp.where(fine_nbr >= coarse_pts, shifted, fine_nbr).astype(jnp.int32)

    def gather_near(neighbours):
        valid = neighbours >= 0
        safe_index = jnp.where(valid, neighbours, 0).astype(jnp.int32)
        values = probe_all[:, safe_index]
        return jnp.where(valid[None], values, jnp.zeros((), values.dtype))

    coarse_res, coarse_own, coarse_near = block_pass(
        coarse_probe.reshape(probes, coarse_blocks, block_len), gather_near(coarse_nbr),
        coarse_diag.reshape(coarse_blocks, block_len, block_len),
        coarse_cond.reshape(coarse_blocks, block_len, slot_count), coarse_nbr >= 0)

    def stretch_pass(pieces):
        own_probe, block_diag, block_cond, neighbours = pieces
        return block_pass(own_probe, gather_near(neighbours), block_diag, block_cond, neighbours >= 0)

    fine_own_in = fine_probe.reshape(probes, stretch_count, FB, block_len).transpose(1, 0, 2, 3)
    fine_res, fine_own, fine_near = lax.map(stretch_pass, (
        fine_own_in,
        fine_diag.reshape(stretch_count, FB, block_len, block_len),
        fine_cond.reshape(stretch_count, FB, block_len, slot_count),
        fine_global.reshape(stretch_count, FB, slot_count)))

    def unchunk(values):
        return values.transpose(1, 0, 2, 3).reshape(probes, fine_pts)

    fine_out = unchunk(fine_res)
    coarse_out = coarse_res.reshape(probes, coarse_pts)
    back_all = jnp.concatenate([coarse_own.reshape(probes, coarse_pts), unchunk(fine_own)], axis=1)
    near_terms = jnp.concatenate([
        coarse_near.reshape(probes, coarse_blocks * slot_count),
        fine_near.transpose(1, 0, 2, 3).reshape(probes, fine_nbr.shape[0] * slot_count)], axis=1)
    all_nbr = jnp.concatenate([coarse_nbr.reshape(-1), fine_global.reshape(-1)])
    safe_all = jnp.where(all_nbr >= 0, all_nbr, 0).astype(jnp.int32)
    back_all = back_all.at[:, safe_all].add(near_terms)
    return fine_out, back_all[:, coarse_pts:], coarse_out, back_all[:, :coarse_pts]
```

```python
import functools

import jax
import jax.numpy as jnp
from jax import lax
from jax.experimental import pallas as pl
from jax.experimental.pallas import tpu as pltpu
from jax.sharding import PartitionSpec as P

RIM = 1024
WIDE = 256
LANES = 128
MESH = pl.DeviceIdType.MESH
NT = (((1,), (1,)), ((), ()))
NN = (((1,), (0,)), ((), ()))
BF = jnp.bfloat16
F32 = jnp.float32


def place():
    grp, tile = lax.axis_index("grp"), lax.axis_index("tile")
    core = tile % 2
    x_hi = (tile // 2) % 2
    y = (tile // 4) % 4
    z = tile // 16
    return grp, z, y, x_hi, core


def dev(grp, z, y, x_hi, core):
    return (grp, ((z * 4 + y) * 2 + x_hi) * 2 + core)


def near_peers(grp, z, y, x_hi, core):
    group = []
    for step in range(1, 8):
        g1, h1, c1 = step // 4, (step // 2) % 2, step % 2
        group.append(((grp + g1) % 2, (x_hi + h1) % 2, (core + c1) % 2))
    return group


def greet(grp, z, y, x_hi, core, others=()):
    barrier = pltpu.get_barrier_semaphore()
    count = 0
    for g1, h1, c1 in near_peers(grp, z, y, x_hi, core):
        pl.semaphore_signal(barrier, inc=1, device_id=dev(g1, z, y, h1, c1), device_id_type=MESH)
        count += 1
    for step in range(1, 8):
        pl.semaphore_signal(
            barrier, inc=1, device_id=dev(grp, (z + step) % 8, y, x_hi, core), device_id_type=MESH
        )
        count += 1
    for step in range(1, 4):
        pl.semaphore_signal(
            barrier, inc=1, device_id=dev(grp, z, (y + step) % 4, x_hi, core), device_id_type=MESH
        )
        count += 1
    for other in others:
        pl.semaphore_signal(barrier, inc=1, device_id=other, device_id_type=MESH)
        count += 1
    pl.semaphore_wait(barrier, count)


def lane_part(ref_value, which):
    return ref_value[:, which * 32 : which * 32 + 32]


def gather_kernel(shard_ref, fine_ref, all_ref, rim_ref, got, s1, r1, s2, r2, s3, r3, s4, r4, s5, r5):
    grp, z, y, x_hi, core = place()
    tile = lax.axis_index("tile")
    tiles = lax.axis_size("tile")
    right = (grp, (tile + 1) % tiles)
    left = (grp, (tile + tiles - 1) % tiles)
    spot = grp * 4 + x_hi * 2 + core
    wide = shard_ref[...]
    got[spot] = jnp.concatenate([wide] * 4, axis=1)
    greet(grp, z, y, x_hi, core, (left, right))
    first = []
    for k, (g1, h1, c1) in enumerate(near_peers(grp, z, y, x_hi, core)):
        part = got.at[spot, pl.ds(pl.multiple_of(c1 * 32, 32), 32), :]
        copy = pltpu.make_async_remote_copy(
            src_ref=part, dst_ref=part, send_sem=s1.at[k], recv_sem=r1.at[k],
            device_id=dev(g1, z, y, h1, c1), device_id_type=MESH,
        )
        copy.start()
        first.append(copy)
    rim = pltpu.make_async_remote_copy(
        src_ref=fine_ref.at[:, pl.ds(fine_ref.shape[1] - RIM, RIM)], dst_ref=rim_ref,
        send_sem=s5, recv_sem=r5, device_id=right, device_id_type=MESH,
    )
    rim.start()
    for copy in first:
        copy.wait()
    rows = pl.ds(pl.multiple_of(core * 32, 32), 32)
    lane = lax.broadcasted_iota(jnp.int32, (32, LANES), 1) // 32
    y_hi, y_at = y // 2, pl.multiple_of((y % 2) * LANES, LANES)
    for g in range(2):
        chunk = got[g * 4, rows, :].astype(F32)
        for k in range(1, 4):
            chunk = jnp.where(lane == k, got[g * 4 + k, rows, :].astype(F32), chunk)
        all_ref[g, z, y_hi, rows, pl.ds(y_at, LANES)] = chunk.astype(BF)
    lanes = pl.ds(y_at, LANES)
    second = []
    for k in range(7):
        part = all_ref.at[:, z, y_hi, rows, lanes]
        copy = pltpu.make_async_remote_copy(
            src_ref=part, dst_ref=part, send_sem=s2.at[k], recv_sem=r2.at[k],
            device_id=dev(grp, (z + k + 1) % 8, y, x_hi, core), device_id_type=MESH,
        )
        copy.start()
        second.append(copy)
    for copy in second:
        copy.wait()
    part = all_ref.at[:, :, y_hi, rows, lanes]
    third = []
    for k in range(3):
        copy = pltpu.make_async_remote_copy(
            src_ref=part, dst_ref=part, send_sem=s3.at[k], recv_sem=r3.at[k],
            device_id=dev(grp, z, (y + k + 1) % 4, x_hi, core), device_id_type=MESH,
        )
        copy.start()
        third.append(copy)
    swap = []
    sibling = dev(grp, z, y, x_hi, 1 - core)
    for k in range(4):
        if k > 0:
            third[k - 1].wait()
        from_y = (y + 4 - k) % 4
        part = all_ref.at[:, :, from_y // 2, rows, pl.ds(pl.multiple_of((from_y % 2) * LANES, LANES), LANES)]
        copy = pltpu.make_async_remote_copy(
            src_ref=part, dst_ref=part, send_sem=s4.at[k], recv_sem=r4.at[k],
            device_id=sibling, device_id_type=MESH,
        )
        copy.start()
        swap.append(copy)
    for copy in swap:
        copy.wait()
    rim.wait()


def gather_call(coarse_probe, fine_probe):
    vmem = pl.BlockSpec(memory_space=pltpu.VMEM)
    dma = pltpu.SemaphoreType.DMA
    return pl.pallas_call(
        gather_kernel,
        name="coarse_gather",
        out_shape=(
            jax.ShapeDtypeStruct((2, 8, 2, 64, WIDE), BF),
            jax.ShapeDtypeStruct((64, RIM), BF),
        ),
        in_specs=[vmem, pl.BlockSpec(memory_space=pl.ANY)],
        out_specs=(vmem, vmem),
        scratch_shapes=[
            pltpu.VMEM((8, 64, LANES), BF),
            dma((7,)), dma((7,)), dma((7,)), dma((7,)), dma((3,)), dma((3,)), dma((4,)), dma((4,)),
            dma, dma,
        ],
        compiler_params=pltpu.CompilerParams(collective_id=0, has_side_effects=True),
    )(coarse_probe, fine_probe)


def sum_kernel(
    terms_ref, rim_ref, back_ref, rim_out_ref,
    half_out, half_in, acc, y_out, y_in, z_out, z_in, x_out, x_in,
    s1, r1, s2, r2, s3, r3, s4, r4, s5, r5,
):
    grp, z, y, x_hi, core = place()
    tile = lax.axis_index("tile")
    tiles = lax.axis_size("tile")
    right = (grp, (tile + 1) % tiles)
    left = (grp, (tile + tiles - 1) % tiles)
    mine = pl.multiple_of(core * 32, 32)
    other = pl.multiple_of((1 - core) * 32, 32)

    @pl.loop(0, 32)
    def _(k):
        half_out[k] = terms_ref[k, pl.ds(other, 32), :].astype(BF)

    greet(grp, z, y, x_hi, core, (left, right))
    swap = pltpu.make_async_remote_copy(
        src_ref=half_out, dst_ref=half_in, send_sem=s1, recv_sem=r1,
        device_id=dev(grp, z, y, x_hi, 1 - core), device_id_type=MESH,
    )
    swap.start()
    rim = pltpu.make_async_remote_copy(
        src_ref=rim_ref, dst_ref=rim_out_ref, send_sem=s5, recv_sem=r5,
        device_id=left, device_id_type=MESH,
    )
    rim.start()
    swap.wait()

    @pl.loop(0, 16)
    def _(gz):
        for y_hi in range(2):
            k = gz * 2 + y_hi
            total = terms_ref[k, pl.ds(mine, 32), :] + half_in[k].astype(F32)
            for y_lo in range(2):
                piece = total[:, y_lo * LANES : y_lo * LANES + LANES]
                acc[y_hi * 2 + y_lo, gz] = piece
                y_out[y_hi * 2 + y_lo, gz] = piece.astype(BF)

    first = []
    for k in range(3):
        copy = pltpu.make_async_remote_copy(
            src_ref=y_out.at[(y + k + 1) % 4], dst_ref=y_in.at[k], send_sem=s2.at[k], recv_sem=r2.at[k],
            device_id=dev(grp, z, (y + k + 1) % 4, x_hi, core), device_id_type=MESH,
        )
        copy.start()
        first.append(copy)
    for copy in first:
        copy.wait()

    @pl.loop(0, 8)
    def _(zz):
        for g in range(2):
            gz = g * 8 + zz
            total = acc[y, gz]
            for k in range(3):
                total = total + y_in[k, gz].astype(F32)
            acc[y, gz] = total
            z_out[zz, g] = total.astype(BF)

    second = []
    for k in range(7):
        copy = pltpu.make_async_remote_copy(
            src_ref=z_out.at[(z + k + 1) % 8], dst_ref=z_in.at[k], send_sem=s3.at[k], recv_sem=r3.at[k],
            device_id=dev(grp, (z + k + 1) % 8, y, x_hi, core), device_id_type=MESH,
        )
        copy.start()
        second.append(copy)
    for copy in second:
        copy.wait()
    for g in range(2):
        total = acc[y, g * 8 + z]
        for k in range(7):
            total = total + z_in[k, g].astype(F32)
        x_out[g] = total
    third = []
    spot = grp * 4 + x_hi * 2 + core
    for k, (g1, h1, c1) in enumerate(near_peers(grp, z, y, x_hi, core)):
        copy = pltpu.make_async_remote_copy(
            src_ref=x_out.at[g1], dst_ref=x_in.at[spot], send_sem=s4.at[k], recv_sem=r4.at[k],
            device_id=dev(g1, z, y, h1, c1), device_id_type=MESH,
        )
        copy.start()
        third.append(copy)
    x_in[spot] = x_out[grp]
    for copy in third:
        copy.wait()
    which = x_hi * 2 + core
    for half in range(2):
        total = (x_in[half] + x_in[2 + half]) + (x_in[4 + half] + x_in[6 + half])
        part = lane_part(total, 0)
        for k in range(1, 4):
            part = jnp.where(which == k, lane_part(total, k), part)
        back_ref[half * 32 : half * 32 + 32, :] = part
    rim.wait()


def sum_call(terms, rim_terms):
    vmem = pl.BlockSpec(memory_space=pltpu.VMEM)
    dma = pltpu.SemaphoreType.DMA
    return pl.pallas_call(
        sum_kernel,
        name="coarse_sum",
        out_shape=(
            jax.ShapeDtypeStruct((64, 32), F32),
            jax.ShapeDtypeStruct((64, RIM), BF),
        ),
        in_specs=[vmem, vmem],
        out_specs=(vmem, vmem),
        scratch_shapes=[
            pltpu.VMEM((32, 32, WIDE), BF),
            pltpu.VMEM((32, 32, WIDE), BF),
            pltpu.VMEM((4, 16, 32, LANES), F32),
            pltpu.VMEM((4, 16, 32, LANES), BF),
            pltpu.VMEM((3, 16, 32, LANES), BF),
            pltpu.VMEM((8, 2, 32, LANES), BF),
            pltpu.VMEM((7, 2, 32, LANES), BF),
            pltpu.VMEM((2, 32, LANES), F32),
            pltpu.VMEM((8, 32, LANES), F32),
            dma, dma, dma((3,)), dma((3,)), dma((7,)), dma((7,)), dma((7,)), dma((7,)), dma, dma,
        ],
        compiler_params=pltpu.CompilerParams(collective_id=1, has_side_effects=True),
    )(terms, rim_terms)


LO = 8
GROUP = 4


def one_hot(hi):
    spots = lax.broadcasted_iota(jnp.int32, (WIDE, WIDE), 0)
    return jnp.where(spots == hi, jnp.float32(1), jnp.float32(0)).astype(BF)


def dot(a, b, dims):
    return lax.dot_general(a, b, dims, preferred_element_type=F32)


def picked(rows, hot, lo, first, acc):
    found = dot(rows, hot, NN)
    for j in range(LO):
        acc = jnp.where(lo == first + j, found[j * 64 : j * 64 + 64], acc)
    return acc


def spread(terms, lo, first):
    zero = jnp.zeros_like(terms)
    parts = [jnp.where(lo == first + j, terms, zero).astype(BF) for j in range(LO)]
    return jnp.concatenate(parts, axis=0)


def halves(a, b):
    lane = lax.broadcasted_iota(jnp.int32, a.shape, 1)
    low = lane < 64
    return (
        jnp.where(low, a, pltpu.roll(b, 64, 1)),
        jnp.where(low, pltpu.roll(a, 64, 1), b),
    )


def coarse_rows(all_ref, first):
    return jnp.concatenate([all_ref[first + j] for j in range(LO)], axis=0)


def coarse_pick(all_ref, hot, lo):
    acc = jnp.zeros((64, WIDE), F32)
    for m in range(32 // LO):
        acc = picked(coarse_rows(all_ref, m * LO), hot, lo, m * LO, acc)
    return acc


def block_kernel(
    all_ref, rim_ref, fine_ref, nbr_ref, diag_ref, cond_ref, cdiag_ref, ccond_ref, clinks_ref,
    out_ref, back_ref, cout_ref, terms_ref, rim_terms_ref,
    ctx, totals, cterms, clo, chi, own_back,
):
    g = pl.program_id(0)
    steps = pl.num_programs(0)
    block = lax.axis_index("grp") * (lax.axis_size("tile") // 4) + lax.axis_index("tile") // 4
    pts = fine_ref.shape[1]

    @pl.when(g == 0)
    def _():
        ctx[:, 0:RIM] = rim_ref[...]
        ctx[:, RIM : RIM + pts] = fine_ref[...]
        ctx[:, RIM + pts :] = jnp.zeros((64, ctx.shape[1] - RIM - pts), BF)
        totals[...] = jnp.zeros_like(totals)
        links = jnp.concatenate(
            [clinks_ref[pl.ds(block, 1), :], jnp.full((1, LANES), -1, jnp.int32)], axis=1
        )
        lo, hi = links >> 8, links & 255
        near = coarse_pick(all_ref, one_hot(hi), lo)[:, :LANES].astype(BF)
        pair = all_ref[block // 2]
        own = jnp.where(block % 2 == 1, pair[:, LANES:].astype(F32), pair[:, :LANES].astype(F32)).astype(BF)
        res = (dot(own, cdiag_ref[...], NT) + dot(near, ccond_ref[...], NT)).astype(BF)
        cout_ref[...] = res
        own_back[...] = dot(res, cdiag_ref[...], NN)
        terms = dot(res, ccond_ref[...], NN)
        cterms[steps] = jnp.concatenate([terms, jnp.zeros_like(terms)], axis=1)
        clo[steps] = lo
        chi[steps] = hi

    rows = [nbr_ref[pl.ds(g * GROUP + r, 1), :] for r in range(GROUP)]
    c01, f01 = halves(rows[0], rows[1])
    c23, f23 = halves(rows[2], rows[3])
    cidx = jnp.concatenate([c01, c23], axis=1)
    fidx = jnp.concatenate([f01, f23], axis=1) - 8192
    lo_c, hi_c = cidx >> 8, cidx & 255
    lo_f, hi_f = fidx >> 8, fidx & 255
    clo[g] = lo_c
    chi[g] = hi_c
    near_c = coarse_pick(all_ref, one_hot(hi_c), lo_c)
    hot_f = one_hot(hi_f)
    spans = (2 * g + 6 + LO - 1) // LO

    def pick_step(m, acc):
        at = m * (LO * WIDE)
        lhs = jnp.concatenate(
            [ctx[:, pl.ds(pl.multiple_of(at + j * WIDE, WIDE), WIDE)] for j in range(LO)], axis=0
        )
        return picked(lhs, hot_f, lo_f, m * LO, acc)

    near_f = lax.fori_loop(0, spans, pick_step, jnp.zeros((64, WIDE), F32))
    terms_c, terms_f = [], []
    for pair in range(GROUP // 2):
        lanes = slice(pair * LANES, pair * LANES + LANES)
        nears = halves(near_c[:, lanes], near_f[:, lanes])
        backs = []
        for r in range(2):
            at = (pair * 2 + r) * LANES
            own = ctx[:, pl.ds(pl.multiple_of(RIM + g * (GROUP * LANES) + at, LANES), LANES)]
            diag = diag_ref[at : at + LANES, :]
            cond = cond_ref[at : at + LANES, :]
            res = (dot(own, diag, NT) + dot(nears[r].astype(BF), cond, NT)).astype(BF)
            out_ref[:, at : at + LANES] = res
            where_at = pl.ds(pl.multiple_of(RIM + g * (GROUP * LANES) + at, LANES), LANES)
            totals[:, where_at] = totals[:, where_at] + dot(res, diag, NN)
            backs.append(dot(res, cond, NN))
        tc, tf = halves(backs[0], backs[1])
        terms_c.append(tc)
        terms_f.append(tf)
    cterms[g] = jnp.concatenate(terms_c, axis=1)
    fterms = jnp.concatenate(terms_f, axis=1)

    def spread_step(m, carry):
        found = dot(spread(fterms, lo_f, m * LO), hot_f, NT)
        for j in range(LO):
            where_at = pl.ds(pl.multiple_of(m * (LO * WIDE) + j * WIDE, WIDE), WIDE)
            totals[:, where_at] = totals[:, where_at] + found[j * 64 : j * 64 + 64]
        return carry

    lax.fori_loop(0, spans, spread_step, 0)

    @pl.when(g == steps - 1)
    def _():
        back_ref[...] = totals[:, RIM : RIM + pts]
        rim_terms_ref[...] = totals[:, 0:RIM].astype(BF)

        @pl.loop(0, 32 // LO)
        def _(m):
            def add(k, acc):
                return acc + dot(spread(cterms[k], clo[k], m * LO), one_hot(chi[k]), NT)

            acc = lax.fori_loop(0, steps + 1, add, jnp.zeros((LO * 64, WIDE), F32))
            for j in range(LO):
                terms_ref[m * LO + j] = acc[j * 64 : j * 64 + 64]

        odd = block % 2 == 1
        own = own_back[...]
        none = jnp.zeros_like(own)
        terms_ref[block // 2] = terms_ref[block // 2] + jnp.concatenate(
            [jnp.where(odd, none, own), jnp.where(odd, own, none)], axis=1
        )


def block_call(coarse_all, rim, fine_probe, nbr, diag, cond, cdiag, ccond, clinks):
    pts = fine_probe.shape[1]
    steps = nbr.shape[0] // GROUP
    whole = lambda *shape: pl.BlockSpec(shape, lambda g: (0,) * len(shape))
    span = GROUP * LANES
    wide = -(-(RIM + pts) // (LO * WIDE)) * LO * WIDE
    return pl.pallas_call(
        block_kernel,
        name="blocks",
        grid=(steps,),
        out_shape=(
            jax.ShapeDtypeStruct((64, pts), BF),
            jax.ShapeDtypeStruct((64, pts), F32),
            jax.ShapeDtypeStruct((64, 32), BF),
            jax.ShapeDtypeStruct((32, 64, WIDE), F32),
            jax.ShapeDtypeStruct((64, RIM), BF),
        ),
        in_specs=[
            whole(32, 64, WIDE), whole(64, RIM), whole(64, pts), whole(*nbr.shape),
            pl.BlockSpec((span, LANES), lambda g: (g, 0)),
            pl.BlockSpec((span, LANES), lambda g: (g, 0)),
            whole(32, LANES), whole(32, LANES), whole(64, LANES),
        ],
        out_specs=(
            pl.BlockSpec((64, span), lambda g: (0, g)),
            whole(64, pts), whole(64, 32), whole(32, 64, WIDE), whole(64, RIM),
        ),
        scratch_shapes=[
            pltpu.VMEM((64, wide), BF),
            pltpu.VMEM((64, wide), F32),
            pltpu.VMEM((steps + 1, 64, WIDE), F32),
            pltpu.VMEM((steps + 1, 1, WIDE), jnp.int32),
            pltpu.VMEM((steps + 1, 1, WIDE), jnp.int32),
            pltpu.VMEM((64, LANES), F32),
        ],
        compiler_params=pltpu.CompilerParams(vmem_limit_bytes=50 * 1024 * 1024),
    )(coarse_all, rim, fine_probe, nbr, diag, cond, cdiag, ccond, clinks)


def on_device(
    fine_probe, coarse_probe, fine_diag, fine_cond, fine_nbr, coarse_diag, coarse_cond, coarse_nbr
):
    coarse_all, rim = gather_call(coarse_probe, fine_probe)
    fine_out, fine_back, coarse_out, terms, rim_terms = block_call(
        coarse_all.reshape(32, 64, WIDE), rim, fine_probe, fine_nbr, fine_diag, fine_cond,
        coarse_diag, coarse_cond, coarse_nbr,
    )
    coarse_back, rim_in = sum_call(terms, rim_terms)
    last = lax.axis_index("tile") == lax.axis_size("tile") - 1
    rim_in = jnp.where(last, jnp.zeros((), F32), rim_in.astype(F32))
    fine_back = fine_back.at[:, -RIM:].add(rim_in)
    return fine_out, fine_back, coarse_out, coarse_back


def solution(mesh):
    columns, rows = P(None, ("grp", "tile")), P(("grp", "tile"), None)
    return jax.shard_map(
        on_device,
        mesh=mesh,
        in_specs=(columns, columns, rows, rows, rows, rows, rows, P()),
        out_specs=(columns, columns, columns, columns),
        check_vma=False,
    )
```

```python
import jax
import jax.numpy as jnp
from jax import lax
from jax.experimental import pallas as pl
from jax.experimental.pallas import tpu as pltpu
from jax.sharding import PartitionSpec as P

RIM = 1024
WIDE = 256
LANES = 128
MESH = pl.DeviceIdType.MESH
NT = (((1,), (1,)), ((), ()))
NN = (((1,), (0,)), ((), ()))
TN = (((0,), (0,)), ((), ()))
BF = jnp.bfloat16
F32 = jnp.float32
GROUP = 16
SLOTS = GROUP * 64
PART = 8


def place():
    grp, tile = lax.axis_index("grp"), lax.axis_index("tile")
    core = tile % 2
    x_hi = (tile // 2) % 2
    y = (tile // 4) % 4
    z = tile // 16
    return grp, z, y, x_hi, core


def dev(grp, z, y, x_hi, core):
    return (grp, ((z * 4 + y) * 2 + x_hi) * 2 + core)


def near_peers(grp, z, y, x_hi, core):
    group = []
    for step in range(1, 8):
        g1, h1, c1 = step // 4, (step // 2) % 2, step % 2
        group.append(((grp + g1) % 2, (x_hi + h1) % 2, (core + c1) % 2))
    return group


def greet(grp, z, y, x_hi, core, others=()):
    barrier = pltpu.get_barrier_semaphore()
    count = 0
    for g1, h1, c1 in near_peers(grp, z, y, x_hi, core):
        pl.semaphore_signal(barrier, inc=1, device_id=dev(g1, z, y, h1, c1), device_id_type=MESH)
        count += 1
    for step in range(1, 8):
        pl.semaphore_signal(
            barrier, inc=1, device_id=dev(grp, (z + step) % 8, y, x_hi, core), device_id_type=MESH
        )
        count += 1
    for step in range(1, 4):
        pl.semaphore_signal(
            barrier, inc=1, device_id=dev(grp, z, (y + step) % 4, x_hi, core), device_id_type=MESH
        )
        count += 1
    for other in others:
        pl.semaphore_signal(barrier, inc=1, device_id=other, device_id_type=MESH)
        count += 1
    pl.semaphore_wait(barrier, count)


def gather_kernel(
    shard_ref, fine_ref, nbr_ref, all_ref, near_ref,
    got, ctx, hots, s1, r1, s2, r2, s3, r3, s4, r4, s5, r5, s6,
):
    grp, z, y, x_hi, core = place()
    tile = lax.axis_index("tile")
    tiles = lax.axis_size("tile")
    right = (grp, (tile + 1) % tiles)
    left = (grp, (tile + tiles - 1) % tiles)
    spot = grp * 4 + x_hi * 2 + core
    pts = fine_ref.shape[1]
    groups = nbr_ref.shape[0] // GROUP
    load = pltpu.make_async_copy(fine_ref, ctx.at[:, pl.ds(RIM, pts)], s6)
    load.start()
    lane = lax.broadcasted_iota(jnp.int32, (32, LANES), 1) % 32
    tiled = jnp.where(lane == lax.broadcasted_iota(jnp.int32, (32, LANES), 0), jnp.float32(1), jnp.float32(0))
    got[spot] = dot(shard_ref[...], tiled.astype(BF), TN).astype(BF)
    greet(grp, z, y, x_hi, core, (left, right))
    first = []
    for k, (g1, h1, c1) in enumerate(near_peers(grp, z, y, x_hi, core)):
        part = got.at[spot, pl.ds(pl.multiple_of(c1 * 32, 32), 32), :]
        copy = pltpu.make_async_remote_copy(
            src_ref=part, dst_ref=part, send_sem=s1.at[k], recv_sem=r1.at[k],
            device_id=dev(g1, z, y, h1, c1), device_id_type=MESH,
        )
        copy.start()
        first.append(copy)
    rim = pltpu.make_async_remote_copy(
        src_ref=fine_ref.at[:, pl.ds(pts - RIM, RIM)], dst_ref=ctx.at[:, pl.ds(0, RIM)],
        send_sem=s5, recv_sem=r5, device_id=right, device_id_type=MESH,
    )
    rim.start()
    los = []
    for g in range(groups):
        lo, hi = fine_slots(nbr_ref, g)
        los.append(lo)
        hots[g] = one_hot(hi)
    load.wait()

    def pick_own(g):
        acc = jnp.zeros((64, SLOTS), F32)
        for part in range(g + 1):
            acc = picked(lane_rows(ctx, 4 + part * PART, PART), hots[g], los[g], 4 + part * PART, acc)
        near_ref[g] = acc.astype(BF)

    def pick_rim(g):
        acc = picked(lane_rows(ctx, 0, 4), hots[g], los[g], 0, near_ref[g].astype(F32))
        near_ref[g] = acc.astype(BF)

    pick_own(0)
    pick_own(1)
    for copy in first:
        copy.wait()
    rows = pl.ds(pl.multiple_of(core * 32, 32), 32)
    lane = lax.broadcasted_iota(jnp.int32, (32, LANES), 1) // 32
    y_hi, y_at = y // 2, pl.multiple_of((y % 2) * LANES, LANES)
    for g in range(2):
        chunk = got[g * 4, rows, :].astype(F32)
        for k in range(1, 4):
            chunk = jnp.where(lane == k, got[g * 4 + k, rows, :].astype(F32), chunk)
        all_ref[g, z, y_hi, rows, pl.ds(y_at, LANES)] = chunk.astype(BF)
    lanes = pl.ds(y_at, LANES)
    second = []
    for k in range(7):
        part = all_ref.at[:, z, y_hi, rows, lanes]
        copy = pltpu.make_async_remote_copy(
            src_ref=part, dst_ref=part, send_sem=s2.at[k], recv_sem=r2.at[k],
            device_id=dev(grp, (z + k + 1) % 8, y, x_hi, core), device_id_type=MESH,
        )
        copy.start()
        second.append(copy)
    pick_own(2)
    for copy in second:
        copy.wait()
    part = all_ref.at[:, :, y_hi, rows, lanes]
    third = []
    for k in range(3):
        copy = pltpu.make_async_remote_copy(
            src_ref=part, dst_ref=part, send_sem=s3.at[k], recv_sem=r3.at[k],
            device_id=dev(grp, z, (y + k + 1) % 4, x_hi, core), device_id_type=MESH,
        )
        copy.start()
        third.append(copy)
    swap = []
    sibling = dev(grp, z, y, x_hi, 1 - core)
    for k in range(4):
        if k == 1:
            for g in range(3, groups):
                pick_own(g)
        if k > 0:
            third[k - 1].wait()
        from_y = (y + 4 - k) % 4
        part = all_ref.at[:, :, from_y // 2, rows, pl.ds(pl.multiple_of((from_y % 2) * LANES, LANES), LANES)]
        copy = pltpu.make_async_remote_copy(
            src_ref=part, dst_ref=part, send_sem=s4.at[k], recv_sem=r4.at[k],
            device_id=sibling, device_id_type=MESH,
        )
        copy.start()
        swap.append(copy)
    rim.wait()
    for g in range(groups):
        pick_rim(g)
    for copy in swap:
        copy.wait()


def gather_call(coarse_shard, fine_probe, nbr):
    vmem = pl.BlockSpec(memory_space=pltpu.VMEM)
    dma = pltpu.SemaphoreType.DMA
    groups = nbr.shape[0] // GROUP
    return pl.pallas_call(
        gather_kernel,
        name="coarse_gather",
        out_shape=(
            jax.ShapeDtypeStruct((2, 8, 2, 64, WIDE), BF),
            jax.ShapeDtypeStruct((groups, 64, SLOTS), BF),
        ),
        in_specs=[vmem, pl.BlockSpec(memory_space=pl.ANY), vmem],
        out_specs=(vmem, vmem),
        scratch_shapes=[
            pltpu.VMEM((8, 64, LANES), BF),
            pltpu.VMEM((64, RIM + fine_probe.shape[1]), BF),
            pltpu.VMEM((groups, WIDE, SLOTS), BF),
            dma((7,)), dma((7,)), dma((7,)), dma((7,)), dma((3,)), dma((3,)), dma((4,)), dma((4,)),
            dma, dma, dma,
        ],
        compiler_params=pltpu.CompilerParams(
            collective_id=0, has_side_effects=True, vmem_limit_bytes=60 * 1024 * 1024
        ),
    )(coarse_shard, fine_probe, nbr)


def sum_kernel(
    terms_ref, fterms_ref, nbr_ref, own_ref, back_ref, fine_ref,
    hots, totals, rim_out, rim_in, half_out, half_in, acc, y_out, y_in, z_out, z_in, x_out, x_in,
    s1, r1, s2, r2, s3, r3, s4, r4, s5, r5, s6, s7,
):
    grp, z, y, x_hi, core = place()
    tile = lax.axis_index("tile")
    tiles = lax.axis_size("tile")
    right = (grp, (tile + 1) % tiles)
    left = (grp, (tile + tiles - 1) % tiles)
    mine = pl.multiple_of(core * 32, 32)
    pts = own_ref.shape[1]
    groups = nbr_ref.shape[0] // GROUP
    load = pltpu.make_async_copy(own_ref, totals, s6)
    load.start()
    other = pl.multiple_of((1 - core) * 32, 32)

    @pl.loop(0, 32)
    def _(k):
        half_out[k] = terms_ref[k, pl.ds(other, 32), :].astype(BF)

    greet(grp, z, y, x_hi, core, (left, right))
    swap = pltpu.make_async_remote_copy(
        src_ref=half_out, dst_ref=half_in, send_sem=s1, recv_sem=r1,
        device_id=dev(grp, z, y, x_hi, 1 - core), device_id_type=MESH,
    )
    swap.start()
    los = []
    for g in range(groups):
        lo, hi = fine_slots(nbr_ref, g)
        los.append(lo.astype(BF))
        hots[g] = one_hot(hi)

    def spread_sum(first, parts, start):
        total = None
        for g in range(start, groups):
            found = dot(spread(fterms_ref[g], los[g], first, parts), hots[g], NT)
            total = found if total is None else total + found
        return total

    rim_terms = spread_sum(0, 4, 0)
    for j in range(4):
        rim_out[:, j * WIDE : j * WIDE + WIDE] = rim_terms[j * 64 : j * 64 + 64].astype(BF)
    rim = pltpu.make_async_remote_copy(
        src_ref=rim_out, dst_ref=rim_in, send_sem=s5, recv_sem=r5,
        device_id=left, device_id_type=MESH,
    )
    rim.start()
    stores = []

    def spread_own(part):
        found = spread_sum(4 + part * PART, PART, part)
        for j in range(PART):
            at = (part * PART + j) * WIDE
            totals[:, at : at + WIDE] = totals[:, at : at + WIDE] + found[j * 64 : j * 64 + 64]

    def store_own(part):
        at = pl.ds(part * PART * WIDE, PART * WIDE)
        store = pltpu.make_async_copy(totals.at[:, at], fine_ref.at[:, at], s7.at[part])
        store.start()
        stores.append(store)

    swap.wait()

    @pl.loop(0, 16)
    def _(gz):
        for y_hi in range(2):
            k = gz * 2 + y_hi
            total = terms_ref[k, pl.ds(mine, 32), :] + half_in[k].astype(F32)
            for y_lo in range(2):
                piece = total[:, y_lo * LANES : y_lo * LANES + LANES]
                acc[y_hi * 2 + y_lo, gz] = piece
                y_out[y_hi * 2 + y_lo, gz] = piece.astype(BF)

    first = []
    for k in range(3):
        copy = pltpu.make_async_remote_copy(
            src_ref=y_out.at[(y + k + 1) % 4], dst_ref=y_in.at[k], send_sem=s2.at[k], recv_sem=r2.at[k],
            device_id=dev(grp, z, (y + k + 1) % 4, x_hi, core), device_id_type=MESH,
        )
        copy.start()
        first.append(copy)
    load.wait()
    for part in range(2):
        spread_own(part)
        store_own(part)
    for copy in first:
        copy.wait()

    @pl.loop(0, 8)
    def _(zz):
        for g in range(2):
            gz = g * 8 + zz
            total = acc[y, gz]
            for k in range(3):
                total = total + y_in[k, gz].astype(F32)
            acc[y, gz] = total
            z_out[zz, g] = total.astype(BF)

    second = []
    for k in range(7):
        copy = pltpu.make_async_remote_copy(
            src_ref=z_out.at[(z + k + 1) % 8], dst_ref=z_in.at[k], send_sem=s3.at[k], recv_sem=r3.at[k],
            device_id=dev(grp, (z + k + 1) % 8, y, x_hi, core), device_id_type=MESH,
        )
        copy.start()
        second.append(copy)
    spread_own(2)
    store_own(2)
    for copy in second:
        copy.wait()
    for g in range(2):
        total = acc[y, g * 8 + z]
        for k in range(7):
            total = total + z_in[k, g].astype(F32)
        x_out[g] = total
    third = []
    spot = grp * 4 + x_hi * 2 + core
    for k, (g1, h1, c1) in enumerate(near_peers(grp, z, y, x_hi, core)):
        copy = pltpu.make_async_remote_copy(
            src_ref=x_out.at[g1], dst_ref=x_in.at[spot], send_sem=s4.at[k], recv_sem=r4.at[k],
            device_id=dev(g1, z, y, h1, c1), device_id_type=MESH,
        )
        copy.start()
        third.append(copy)
    x_in[spot] = x_out[grp]
    for part in range(3, groups):
        spread_own(part)
        if part < groups - 1:
            store_own(part)
    rim.wait()
    keep = jnp.where(tile == tiles - 1, jnp.float32(0), jnp.float32(1))
    totals[:, pts - RIM :] = totals[:, pts - RIM :] + rim_in[...].astype(F32) * keep
    store_own(groups - 1)
    for copy in third:
        copy.wait()
    which = x_hi * 2 + core
    total = jnp.concatenate(
        [(x_in[half] + x_in[2 + half]) + (x_in[4 + half] + x_in[6 + half]) for half in range(2)], axis=0
    ).T
    part = total[0:32]
    for k in range(1, 4):
        part = jnp.where(which == k, total[k * 32 : k * 32 + 32], part)
    back_ref[...] = part
    for store in stores:
        store.wait()


def sum_call(terms, fterms, nbr, own_back):
    vmem = pl.BlockSpec(memory_space=pltpu.VMEM)
    away = pl.BlockSpec(memory_space=pl.ANY)
    dma = pltpu.SemaphoreType.DMA
    groups = nbr.shape[0] // GROUP
    return pl.pallas_call(
        sum_kernel,
        name="coarse_sum",
        out_shape=(
            jax.ShapeDtypeStruct((32, 64), F32),
            jax.ShapeDtypeStruct(own_back.shape, F32),
        ),
        in_specs=[vmem, vmem, vmem, away],
        out_specs=(vmem, away),
        scratch_shapes=[
            pltpu.VMEM((groups, WIDE, SLOTS), BF),
            pltpu.VMEM(own_back.shape, F32),
            pltpu.VMEM((64, RIM), BF),
            pltpu.VMEM((64, RIM), BF),
            pltpu.VMEM((32, 32, WIDE), BF),
            pltpu.VMEM((32, 32, WIDE), BF),
            pltpu.VMEM((4, 16, 32, LANES), F32),
            pltpu.VMEM((4, 16, 32, LANES), BF),
            pltpu.VMEM((3, 16, 32, LANES), BF),
            pltpu.VMEM((8, 2, 32, LANES), BF),
            pltpu.VMEM((7, 2, 32, LANES), BF),
            pltpu.VMEM((2, 32, LANES), F32),
            pltpu.VMEM((8, 32, LANES), F32),
            dma, dma, dma((3,)), dma((3,)), dma((7,)), dma((7,)), dma((7,)), dma((7,)), dma, dma, dma,
            dma((groups,)),
        ],
        compiler_params=pltpu.CompilerParams(
            collective_id=1, has_side_effects=True, vmem_limit_bytes=60 * 1024 * 1024
        ),
    )(terms, fterms, nbr, own_back)


def one_hot(hi):
    spots = lax.broadcasted_iota(jnp.int32, (WIDE, hi.shape[1]), 0)
    return jnp.where(spots == hi, jnp.float32(1), jnp.float32(0)).astype(BF)


def dot(a, b, dims):
    return lax.dot_general(a, b, dims, preferred_element_type=F32)


def picked(rows, hot, lo, first, acc):
    found = dot(rows, hot, NN)
    for j in range(found.shape[0] // 64):
        acc = jnp.where(lo == first + j, found[j * 64 : j * 64 + 64], acc)
    return acc


def spread(terms, lo, first, parts):
    zero = jnp.zeros_like(terms)
    return jnp.concatenate([jnp.where(lo == (first + j), terms, zero) for j in range(parts)], axis=0)


def halves(a, b):
    lane = lax.broadcasted_iota(jnp.int32, a.shape, 1)
    low = lane < 64
    return (
        jnp.where(low, a, pltpu.roll(b, 64, 1)),
        jnp.where(low, pltpu.roll(a, 64, 1), b),
    )


def lane_rows(ref, first, parts):
    return jnp.concatenate([ref[:, (first + j) * WIDE : (first + j + 1) * WIDE] for j in range(parts)], axis=0)


def slots(nbr_ref, g, which):
    rows = [nbr_ref[pl.ds(g * GROUP + r, 1), :] for r in range(GROUP)]
    return jnp.concatenate([halves(rows[r], rows[r + 1])[which] for r in range(0, GROUP, 2)], axis=1)


def fine_slots(nbr_ref, g):
    at = slots(nbr_ref, g, 1) - 8192
    return at >> 8, at & 255


def coarse_rows(all_ref, first):
    return jnp.concatenate([all_ref[first + j] for j in range(PART)], axis=0)


def coarse_pick(all_ref, hot, lo):
    acc = jnp.zeros((64, lo.shape[1]), F32)
    for m in range(0, 32, PART):
        acc = picked(coarse_rows(all_ref, m), hot, lo, m, acc)
    return acc


def coarse_spread(terms_ref, terms, lo, hot):
    for m in range(0, 32, PART):
        found = dot(spread(terms, lo, m, PART), hot, NT)
        for j in range(PART):
            terms_ref[m + j] = terms_ref[m + j] + found[j * 64 : j * 64 + 64]


def block_kernel(
    all_ref, near_ref, fine_ref, nbr_ref, diag_ref, cond_ref, cdiag_ref, ccond_ref, clinks_ref,
    out_ref, back_ref, cout_ref, terms_ref, fterms_ref,
):
    g = pl.program_id(0)
    block = lax.axis_index("grp") * (lax.axis_size("tile") // 4) + lax.axis_index("tile") // 4

    @pl.when(g == 0)
    def _():
        terms_ref[...] = jnp.zeros_like(terms_ref)
        links = jnp.concatenate(
            [clinks_ref[pl.ds(block, 1), :], jnp.full((1, LANES), -1, jnp.int32)], axis=1
        )
        lo, hi = links >> 8, links & 255
        hot = one_hot(hi)
        near = coarse_pick(all_ref, hot, lo)[:, :LANES].astype(BF)
        pair = all_ref[block // 2]
        own = jnp.where(block % 2 == 1, pair[:, LANES:].astype(F32), pair[:, :LANES].astype(F32)).astype(BF)
        res = (dot(cdiag_ref[...], own, NT) + dot(ccond_ref[...], near, NT)).astype(BF)
        cout_ref[...] = res
        own = dot(res, cdiag_ref[...], TN)
        terms = dot(res, ccond_ref[...], TN).astype(BF)
        coarse_spread(terms_ref, jnp.concatenate([terms, jnp.zeros_like(terms)], axis=1), lo.astype(BF), hot)
        odd = block % 2 == 1
        none = jnp.zeros_like(own)
        terms_ref[block // 2] = terms_ref[block // 2] + jnp.concatenate(
            [jnp.where(odd, none, own), jnp.where(odd, own, none)], axis=1
        )

    cidx = slots(nbr_ref, g, 0)
    lo_c, hi_c = cidx >> 8, cidx & 255
    hot_c = one_hot(hi_c)
    near_c = coarse_pick(all_ref, hot_c, lo_c).astype(BF)
    near_f = near_ref[...]
    nears, results, backs = [], [], []
    for pair in range(GROUP // 2):
        lanes = slice(pair * LANES, pair * LANES + LANES)
        nears.extend(halves(near_c[:, lanes].astype(F32), near_f[:, lanes].astype(F32)))
    for r in range(GROUP):
        at = r * LANES
        both = jnp.concatenate([diag_ref[at : at + LANES, :], cond_ref[at : at + LANES, :]], axis=1)
        pair = jnp.concatenate([fine_ref[:, at : at + LANES], nears[r].astype(BF)], axis=1)
        results.append(dot(pair, both, NT).astype(BF))
    for r in range(GROUP):
        at = r * LANES
        out_ref[:, at : at + LANES] = results[r]
        both = jnp.concatenate([diag_ref[at : at + LANES, :], cond_ref[at : at + LANES, :]], axis=1)
        back = dot(results[r], both, NN)
        back_ref[:, at : at + LANES] = back[:, :LANES]
        backs.append(back[:, LANES:])
    terms = [halves(backs[r], backs[r + 1]) for r in range(0, GROUP, 2)]
    fterms_ref[...] = jnp.concatenate([pair[1] for pair in terms], axis=1).astype(BF)
    cterms = jnp.concatenate([pair[0] for pair in terms], axis=1).astype(BF)
    coarse_spread(terms_ref, cterms, lo_c.astype(BF), hot_c)


def block_call(coarse_all, near, fine_probe, nbr, diag, cond, cdiag, ccond, clinks):
    pts = fine_probe.shape[1]
    steps = nbr.shape[0] // GROUP
    whole = lambda *shape: pl.BlockSpec(shape, lambda g: (0,) * len(shape))
    span = GROUP * LANES
    columns = pl.BlockSpec((64, span), lambda g: (0, g))
    return pl.pallas_call(
        block_kernel,
        name="blocks",
        grid=(steps,),
        out_shape=(
            jax.ShapeDtypeStruct((64, pts), BF),
            jax.ShapeDtypeStruct((64, pts), F32),
            jax.ShapeDtypeStruct((32, 64), BF),
            jax.ShapeDtypeStruct((32, 64, WIDE), F32),
            jax.ShapeDtypeStruct((steps, 64, SLOTS), BF),
        ),
        in_specs=[
            whole(32, 64, WIDE), pl.BlockSpec((None, 64, SLOTS), lambda g: (g, 0, 0)),
            columns, whole(*nbr.shape),
            pl.BlockSpec((span, LANES), lambda g: (g, 0)),
            pl.BlockSpec((span, LANES), lambda g: (g, 0)),
            whole(32, LANES), whole(32, LANES), whole(64, LANES),
        ],
        out_specs=(
            columns, columns, whole(32, 64), whole(32, 64, WIDE),
            pl.BlockSpec((None, 64, SLOTS), lambda g: (g, 0, 0)),
        ),
        compiler_params=pltpu.CompilerParams(vmem_limit_bytes=60 * 1024 * 1024),
    )(coarse_all, near, fine_probe, nbr, diag, cond, cdiag, ccond, clinks)


def on_device(
    fine_probe, coarse_probe, fine_diag, fine_cond, fine_nbr, coarse_diag, coarse_cond, coarse_nbr
):
    coarse_all, near = gather_call(coarse_probe.T, fine_probe, fine_nbr)
    fine_out, own_back, coarse_out, terms, fine_terms = block_call(
        coarse_all.reshape(32, 64, WIDE), near, fine_probe, fine_nbr, fine_diag, fine_cond,
        coarse_diag, coarse_cond, coarse_nbr,
    )
    coarse_back, fine_back = sum_call(terms, fine_terms, fine_nbr, own_back)
    return fine_out, fine_back, coarse_out.T, coarse_back.T


def solution(mesh):
    columns, rows = P(None, ("grp", "tile")), P(("grp", "tile"), None)
    return jax.shard_map(
        on_device,
        mesh=mesh,
        in_specs=(columns, columns, rows, rows, rows, rows, rows, P()),
        out_specs=(columns, columns, columns, columns),
        check_vma=False,
    )
```

```python
import jax
import jax.numpy as jnp
from jax import lax
from jax.experimental import pallas as pl
from jax.experimental.pallas import tpu as pltpu
from jax.sharding import PartitionSpec as P

RIM = 1024
WIDE = 256
LANES = 128
MESH = pl.DeviceIdType.MESH
NT = (((1,), (1,)), ((), ()))
NN = (((1,), (0,)), ((), ()))
TN = (((0,), (0,)), ((), ()))
BF = jnp.bfloat16
F32 = jnp.float32
GROUP = 16
SLOTS = GROUP * 64
PART = 8


def place():
    grp, tile = lax.axis_index("grp"), lax.axis_index("tile")
    core = tile % 2
    x_hi = (tile // 2) % 2
    y = (tile // 4) % 4
    z = tile // 16
    return grp, z, y, x_hi, core


def dev(grp, z, y, x_hi, core):
    return (grp, ((z * 4 + y) * 2 + x_hi) * 2 + core)


def near_peers(grp, z, y, x_hi, core):
    group = []
    for step in range(1, 8):
        g1, h1, c1 = step // 4, (step // 2) % 2, step % 2
        group.append(((grp + g1) % 2, (x_hi + h1) % 2, (core + c1) % 2))
    return group


def greet(grp, z, y, x_hi, core, others=()):
    barrier = pltpu.get_barrier_semaphore()
    count = 0
    for g1, h1, c1 in near_peers(grp, z, y, x_hi, core):
        pl.semaphore_signal(barrier, inc=1, device_id=dev(g1, z, y, h1, c1), device_id_type=MESH)
        count += 1
    for step in range(1, 8):
        pl.semaphore_signal(
            barrier, inc=1, device_id=dev(grp, (z + step) % 8, y, x_hi, core), device_id_type=MESH
        )
        count += 1
    for step in range(1, 4):
        pl.semaphore_signal(
            barrier, inc=1, device_id=dev(grp, z, (y + step) % 4, x_hi, core), device_id_type=MESH
        )
        count += 1
    for other in others:
        pl.semaphore_signal(barrier, inc=1, device_id=other, device_id_type=MESH)
        count += 1
    pl.semaphore_wait(barrier, count)


def gather_kernel(
    shard_ref, fine_ref, nbr_ref, clinks_ref, near_ref, fnear_ref, extra_ref,
    got, ctx, held, hots, fhots, acc, xacc,
    s1, r1, s2, r2, s3, r3, s4, r4, s5, r5, s6,
):
    grp, z, y, x_hi, core = place()
    tile = lax.axis_index("tile")
    tiles = lax.axis_size("tile")
    right = (grp, (tile + 1) % tiles)
    left = (grp, (tile + tiles - 1) % tiles)
    spot = grp * 4 + x_hi * 2 + core
    pts = fine_ref.shape[1]
    groups = nbr_ref.shape[0] // GROUP
    load = pltpu.make_async_copy(fine_ref, ctx.at[:, pl.ds(RIM, pts)], s6)
    load.start()
    lane = lax.broadcasted_iota(jnp.int32, (32, LANES), 1) % 32
    tiled = jnp.where(lane == lax.broadcasted_iota(jnp.int32, (32, LANES), 0), jnp.float32(1), jnp.float32(0))
    got[spot] = dot(shard_ref[...], tiled.astype(BF), TN).astype(BF)
    greet(grp, z, y, x_hi, core, (left, right))
    first = []
    for k, (g1, h1, c1) in enumerate(near_peers(grp, z, y, x_hi, core)):
        part = got.at[spot, pl.ds(pl.multiple_of(c1 * 32, 32), 32), :]
        copy = pltpu.make_async_remote_copy(
            src_ref=part, dst_ref=part, send_sem=s1.at[k], recv_sem=r1.at[k],
            device_id=dev(g1, z, y, h1, c1), device_id_type=MESH,
        )
        copy.start()
        first.append(copy)
    rim = pltpu.make_async_remote_copy(
        src_ref=fine_ref.at[:, pl.ds(pts - RIM, RIM)], dst_ref=ctx.at[:, pl.ds(0, RIM)],
        send_sem=s5, recv_sem=r5, device_id=right, device_id_type=MESH,
    )
    rim.start()
    flos, los = [], []
    for g in range(groups):
        lo, hi = fine_slots(nbr_ref, g)
        flos.append(lo)
        fhots[g] = one_hot(hi)
    load.wait()

    def pick_own(g):
        found = jnp.zeros((64, SLOTS), F32)
        for part in range(g + 1):
            found = picked(lane_rows(ctx, 4 + part * PART, PART), fhots[g], flos[g], 4 + part * PART, found)
        fnear_ref[g] = found.astype(BF)

    def pick_rim(g):
        found = picked(lane_rows(ctx, 0, 4), fhots[g], flos[g], 0, fnear_ref[g].astype(F32))
        fnear_ref[g] = found.astype(BF)

    pick_own(0)
    pick_own(1)
    for copy in first:
        copy.wait()
    rows = pl.ds(pl.multiple_of(core * 32, 32), 32)
    lane = lax.broadcasted_iota(jnp.int32, (32, LANES), 1) // 32
    for g in range(2):
        chunk = got[g * 4, rows, :].astype(F32)
        for k in range(1, 4):
            chunk = jnp.where(lane == k, got[g * 4 + k, rows, :].astype(F32), chunk)
        held[z, y, core, :, g * LANES : g * LANES + LANES] = chunk.astype(BF)
    along_z, along_y, swap = {}, {}, {}
    for dz in (4, 3, 5, 2, 6, 1, 7):
        part = held.at[z, y, core]
        along_z[dz] = pltpu.make_async_remote_copy(
            src_ref=part, dst_ref=part, send_sem=s2.at[dz - 1], recv_sem=r2.at[dz - 1],
            device_id=dev(grp, (z + dz) % 8, y, x_hi, core), device_id_type=MESH,
        )
        along_z[dz].start()

    def send_y(dz):
        if dz > 0:
            along_z[dz].wait()
        for k in (1, 0, 2):
            part = held.at[(z + 8 - dz) % 8, y, core]
            copy = pltpu.make_async_remote_copy(
                src_ref=part, dst_ref=part, send_sem=s3.at[dz, k], recv_sem=r3.at[dz, k],
                device_id=dev(grp, z, (y + k + 1) % 4, x_hi, core), device_id_type=MESH,
            )
            copy.start()
            along_y[dz, k] = copy

    def send_swap(dz):
        for k in range(3):
            along_y[dz, k].wait()
        part = held.at[(z + 8 - dz) % 8, :, core]
        swap[dz] = pltpu.make_async_remote_copy(
            src_ref=part, dst_ref=part, send_sem=s4.at[dz], recv_sem=r4.at[dz],
            device_id=dev(grp, z, y, x_hi, 1 - core), device_id_type=MESH,
        )
        swap[dz].start()

    def pick_coarse(pair, start, end):
        origins = [(z + 8 - dz) % 8 for dz in pair]
        for dz in pair:
            swap[dz].wait()
        lhs = jnp.concatenate([held[origin].reshape(WIDE, WIDE) for origin in origins], axis=0)

        def choose(hot, lo, found):
            hits = dot(lhs, hot, NN)
            for j, origin in enumerate(origins):
                for yy in range(4):
                    at = (j * 4 + yy) * 64
                    found = jnp.where(lo == origin * 4 + yy, hits[at : at + 64], found)
            return found

        for g in range(groups):
            found = choose(hots[g], los[g], jnp.zeros((64, SLOTS), F32) if start else acc[g])
            if end:
                near_ref[g] = found.astype(BF)
            else:
                acc[g] = found
        found = choose(xhot, xlo, jnp.zeros((64, LANES), F32) if start else xacc[...])
        if end:
            extra_ref[0] = found.astype(BF)
        else:
            xacc[...] = found

    send_y(0)
    for g in range(groups):
        lo, hi = coarse_slots(slots(nbr_ref, g, 0))
        los.append(lo)
        hots[g] = one_hot(hi)
    xlo, xhi = coarse_slots(clinks_ref[pl.ds(grp * (tiles // 4) + tile // 4, 1), :])
    xhot = one_hot(xhi)
    pick_own(2)
    send_y(1)
    send_y(7)
    pick_own(3)
    send_y(2)
    send_y(6)
    send_swap(0)
    for g in range(4, groups):
        pick_own(g)
    send_y(3)
    send_y(5)
    send_swap(1)
    send_swap(7)
    rim.wait()
    for g in range(groups):
        pick_rim(g)
    send_y(4)
    send_swap(2)
    send_swap(6)
    pick_coarse((0, 1), True, False)
    send_swap(3)
    send_swap(5)
    pick_coarse((7, 2), False, False)
    send_swap(4)
    pick_coarse((6, 3), False, False)
    pick_coarse((5, 4), False, True)
    own = held[z, y].reshape(64, WIDE)
    extra_ref[1] = jnp.where(grp == 1, own[:, LANES:].astype(F32), own[:, :LANES].astype(F32)).astype(BF)


def gather_call(coarse_shard, fine_probe, nbr, clinks):
    vmem = pl.BlockSpec(memory_space=pltpu.VMEM)
    dma = pltpu.SemaphoreType.DMA
    groups = nbr.shape[0] // GROUP
    near = jax.ShapeDtypeStruct((groups, 64, SLOTS), BF)
    return pl.pallas_call(
        gather_kernel,
        name="coarse_gather",
        out_shape=(near, near, jax.ShapeDtypeStruct((2, 64, LANES), BF)),
        in_specs=[vmem, pl.BlockSpec(memory_space=pl.ANY), vmem, vmem],
        out_specs=(vmem, vmem, vmem),
        scratch_shapes=[
            pltpu.VMEM((8, 64, LANES), BF),
            pltpu.VMEM((64, RIM + fine_probe.shape[1]), BF),
            pltpu.VMEM((8, 4, 2, 32, WIDE), BF),
            pltpu.VMEM((groups, WIDE, SLOTS), BF),
            pltpu.VMEM((groups, WIDE, SLOTS), BF),
            pltpu.VMEM((groups, 64, SLOTS), F32),
            pltpu.VMEM((64, LANES), F32),
            dma((7,)), dma((7,)), dma((7,)), dma((7,)), dma((8, 3)), dma((8, 3)), dma((8,)), dma((8,)),
            dma, dma, dma,
        ],
        compiler_params=pltpu.CompilerParams(
            collective_id=0, has_side_effects=True, vmem_limit_bytes=60 * 1024 * 1024
        ),
    )(coarse_shard, fine_probe, nbr, clinks)


def sum_kernel(
    terms_ref, fterms_ref, extra_ref, xown_ref, nbr_ref, clinks_ref, own_ref, back_ref, fine_ref, rim_in,
    hots, fhots, totals, rim_out, piece, half_out, half_in, acc, y_out, y_in, z_out, z_in, x_out, x_in,
    s1, r1, s2, r2, s3, r3, s4, r4, s5, r5, s6, s7,
):
    grp, z, y, x_hi, core = place()
    tile = lax.axis_index("tile")
    tiles = lax.axis_size("tile")
    right = (grp, (tile + 1) % tiles)
    left = (grp, (tile + tiles - 1) % tiles)
    mine = pl.ds(pl.multiple_of(core * 32, 32), 32)
    other = pl.ds(pl.multiple_of((1 - core) * 32, 32), 32)
    groups = nbr_ref.shape[0] // GROUP
    load = pltpu.make_async_copy(own_ref, totals, s6)
    load.start()
    los, flos = [], []
    for g in range(groups):
        lo, hi = coarse_slots(slots(nbr_ref, g, 0))
        los.append(lo.astype(BF))
        hots[g] = one_hot(hi)
    xlo, xhi = coarse_slots(clinks_ref[pl.ds(grp * (tiles // 4) + tile // 4, 1), :])
    xlo = xlo.astype(BF)
    xhot = one_hot(xhi)
    swap, along_y, along_z = {}, {}, {}

    def spread_coarse(pair):
        targets = [(z + dz) % 8 for dz in pair]

        def lay(terms, lo):
            zero = jnp.zeros_like(terms)
            return jnp.concatenate(
                [jnp.where(lo == (target * 4 + yy).astype(F32).astype(BF), terms, zero)
                 for target in targets for yy in range(4)],
                axis=0,
            )

        total = dot(lay(extra_ref[...], xlo), xhot, NT)
        for g in range(groups):
            total = total + dot(lay(terms_ref[g], los[g]), hots[g], NT)
        for j, dz in enumerate(pair):
            for yy in range(4):
                at = (j * 4 + yy) * 64
                part = total[at : at + 64]
                if dz == 0:
                    own, none = xown_ref[...], jnp.zeros((64, LANES), F32)
                    here = y == yy
                    part = part + jnp.concatenate(
                        [jnp.where(here & (grp == 0), own, none), jnp.where(here & (grp == 1), own, none)], axis=1
                    )
                piece[dz, yy] = part
                half_out[dz, yy] = piece[dz, yy, other, :].astype(BF)

    def send_swap(dz):
        swap[dz] = pltpu.make_async_remote_copy(
            src_ref=half_out.at[dz], dst_ref=half_in.at[dz], send_sem=s1.at[dz], recv_sem=r1.at[dz],
            device_id=dev(grp, z, y, x_hi, 1 - core), device_id_type=MESH,
        )
        swap[dz].start()

    def send_y(dz):
        swap[dz].wait()
        for yy in range(4):
            total = piece[dz, yy, mine, :] + half_in[dz, yy].astype(F32)
            acc[dz, yy] = total
            y_out[dz, yy] = total.astype(BF)
        for k in (1, 0, 2):
            copy = pltpu.make_async_remote_copy(
                src_ref=y_out.at[dz, (y + k + 1) % 4], dst_ref=y_in.at[dz, k],
                send_sem=s2.at[dz, k], recv_sem=r2.at[dz, k],
                device_id=dev(grp, z, (y + k + 1) % 4, x_hi, core), device_id_type=MESH,
            )
            copy.start()
            along_y[dz, k] = copy

    def send_z(dz):
        total = acc[dz, y]
        for k in range(3):
            along_y[dz, k].wait()
            total = total + y_in[dz, k].astype(F32)
        if dz == 0:
            return total
        z_out[dz - 1] = total.astype(BF)
        along_z[dz] = pltpu.make_async_remote_copy(
            src_ref=z_out.at[dz - 1], dst_ref=z_in.at[dz - 1], send_sem=s3.at[dz - 1], recv_sem=r3.at[dz - 1],
            device_id=dev(grp, (z + dz) % 8, y, x_hi, core), device_id_type=MESH,
        )
        along_z[dz].start()

    def spread_sum(first, parts, start):
        total = None
        for g in range(start, groups):
            found = dot(spread(fterms_ref[g], flos[g], first, parts), fhots[g], NT)
            total = found if total is None else total + found
        return total

    stores = []

    def spread_own(part):
        found = spread_sum(4 + part * PART, PART, part)
        for j in range(PART):
            at = (part * PART + j) * WIDE
            totals[:, at : at + WIDE] = totals[:, at : at + WIDE] + found[j * 64 : j * 64 + 64]
        at = pl.ds(part * PART * WIDE, PART * WIDE)
        store = pltpu.make_async_copy(totals.at[:, at], fine_ref.at[:, at], s7.at[part])
        store.start()
        stores.append(store)

    spread_coarse((4, 3))
    greet(grp, z, y, x_hi, core, (left, right))
    send_swap(4)
    send_swap(3)
    spread_coarse((5, 2))
    send_swap(5)
    send_swap(2)
    send_y(4)
    send_y(3)
    spread_coarse((6, 1))
    send_swap(6)
    send_swap(1)
    send_y(5)
    send_y(2)
    spread_coarse((7, 0))
    send_swap(7)
    send_swap(0)
    send_y(6)
    send_y(1)
    send_z(4)
    send_z(3)
    for g in range(groups):
        lo, hi = fine_slots(nbr_ref, g)
        flos.append(lo.astype(BF))
        fhots[g] = one_hot(hi)
    send_y(7)
    send_y(0)
    send_z(5)
    send_z(2)
    rim_terms = spread_sum(0, 4, 0)
    for j in range(4):
        rim_out[:, j * WIDE : j * WIDE + WIDE] = rim_terms[j * 64 : j * 64 + 64].astype(BF)
    rim = pltpu.make_async_remote_copy(
        src_ref=rim_out, dst_ref=rim_in, send_sem=s5, recv_sem=r5,
        device_id=left, device_id_type=MESH,
    )
    rim.start()
    send_z(6)
    send_z(1)
    load.wait()
    spread_own(0)
    send_z(7)
    total = send_z(0)
    spread_own(1)
    for dz in (4, 3, 5, 2, 6, 1, 7):
        along_z[dz].wait()
        total = total + z_in[dz - 1].astype(F32)
    for g in range(2):
        x_out[g] = total[:, g * LANES : g * LANES + LANES]
    third = []
    spot = grp * 4 + x_hi * 2 + core
    for k, (g1, h1, c1) in enumerate(near_peers(grp, z, y, x_hi, core)):
        copy = pltpu.make_async_remote_copy(
            src_ref=x_out.at[g1], dst_ref=x_in.at[spot], send_sem=s4.at[k], recv_sem=r4.at[k],
            device_id=dev(g1, z, y, h1, c1), device_id_type=MESH,
        )
        copy.start()
        third.append(copy)
    x_in[spot] = x_out[grp]
    for part in range(2, groups):
        spread_own(part)
    rim.wait()
    for copy in third:
        copy.wait()
    which = x_hi * 2 + core
    total = jnp.concatenate(
        [(x_in[half] + x_in[2 + half]) + (x_in[4 + half] + x_in[6 + half]) for half in range(2)], axis=0
    ).T
    part = total[0:32]
    for k in range(1, 4):
        part = jnp.where(which == k, total[k * 32 : k * 32 + 32], part)
    back_ref[...] = part
    for store in stores:
        store.wait()


def sum_call(terms, fterms, xterms, xown, nbr, clinks, own_back):
    vmem = pl.BlockSpec(memory_space=pltpu.VMEM)
    away = pl.BlockSpec(memory_space=pl.ANY)
    dma = pltpu.SemaphoreType.DMA
    groups = nbr.shape[0] // GROUP
    return pl.pallas_call(
        sum_kernel,
        name="coarse_sum",
        out_shape=(
            jax.ShapeDtypeStruct((32, 64), F32),
            jax.ShapeDtypeStruct(own_back.shape, F32),
            jax.ShapeDtypeStruct((64, RIM), BF),
        ),
        in_specs=[vmem] * 6 + [away],
        out_specs=(vmem, away, vmem),
        scratch_shapes=[
            pltpu.VMEM((groups, WIDE, SLOTS), BF),
            pltpu.VMEM((groups, WIDE, SLOTS), BF),
            pltpu.VMEM(own_back.shape, F32),
            pltpu.VMEM((64, RIM), BF),
            pltpu.VMEM((8, 4, 64, WIDE), F32),
            pltpu.VMEM((8, 4, 32, WIDE), BF),
            pltpu.VMEM((8, 4, 32, WIDE), BF),
            pltpu.VMEM((8, 4, 32, WIDE), F32),
            pltpu.VMEM((8, 4, 32, WIDE), BF),
            pltpu.VMEM((8, 3, 32, WIDE), BF),
            pltpu.VMEM((7, 32, WIDE), BF),
            pltpu.VMEM((7, 32, WIDE), BF),
            pltpu.VMEM((2, 32, LANES), F32),
            pltpu.VMEM((8, 32, LANES), F32),
            dma((8,)), dma((8,)), dma((8, 3)), dma((8, 3)), dma((7,)), dma((7,)), dma((7,)), dma((7,)),
            dma, dma, dma, dma((groups,)),
        ],
        compiler_params=pltpu.CompilerParams(
            collective_id=1, has_side_effects=True, vmem_limit_bytes=60 * 1024 * 1024
        ),
    )(terms, fterms, xterms, xown, nbr, clinks, own_back)


def one_hot(hi):
    spots = lax.broadcasted_iota(jnp.int32, (WIDE, hi.shape[1]), 0)
    return jnp.where(spots == hi, jnp.float32(1), jnp.float32(0)).astype(BF)


def dot(a, b, dims):
    return lax.dot_general(a, b, dims, preferred_element_type=F32)


def picked(rows, hot, lo, first, acc):
    found = dot(rows, hot, NN)
    for j in range(found.shape[0] // 64):
        acc = jnp.where(lo == first + j, found[j * 64 : j * 64 + 64], acc)
    return acc


def spread(terms, lo, first, parts):
    zero = jnp.zeros_like(terms)
    return jnp.concatenate([jnp.where(lo == (first + j), terms, zero) for j in range(parts)], axis=0)


def halves(a, b):
    lane = lax.broadcasted_iota(jnp.int32, a.shape, 1)
    low = lane < 64
    return (
        jnp.where(low, a, pltpu.roll(b, 64, 1)),
        jnp.where(low, pltpu.roll(a, 64, 1), b),
    )


def lane_rows(ref, first, parts):
    return jnp.concatenate([ref[:, (first + j) * WIDE : (first + j + 1) * WIDE] for j in range(parts)], axis=0)


def slots(nbr_ref, g, which):
    rows = [nbr_ref[pl.ds(g * GROUP + r, 1), :] for r in range(GROUP)]
    return jnp.concatenate([halves(rows[r], rows[r + 1])[which] for r in range(0, GROUP, 2)], axis=1)


def fine_slots(nbr_ref, g):
    at = slots(nbr_ref, g, 1) - 8192
    return at >> 8, at & 255


def coarse_slots(at):
    lo = jnp.where(at < 0, -1, (at >> 7) & 31)
    return lo, ((at >> 12) << 7) + (at & 127)


def block_kernel(
    near_ref, fnear_ref, extra_ref, fine_ref, diag_ref, cond_ref, cdiag_ref, ccond_ref,
    out_ref, back_ref, cout_ref, terms_ref, fterms_ref, xterms_ref, xown_ref,
):
    g = pl.program_id(0)

    @pl.when(g == 0)
    def _():
        res = dot(cdiag_ref[...], extra_ref[1], NT) + dot(ccond_ref[...], extra_ref[0], NT)
        res = res.astype(BF)
        cout_ref[...] = res
        xown_ref[...] = dot(res, cdiag_ref[...], TN)
        xterms_ref[...] = dot(res, ccond_ref[...], TN).astype(BF)

    nears, results, backs = [], [], []
    for pair in range(GROUP // 2):
        lanes = slice(pair * LANES, pair * LANES + LANES)
        nears.extend(halves(near_ref[:, lanes].astype(F32), fnear_ref[:, lanes].astype(F32)))
    for r in range(GROUP):
        at = r * LANES
        both = jnp.concatenate([diag_ref[at : at + LANES, :], cond_ref[at : at + LANES, :]], axis=1)
        pair = jnp.concatenate([fine_ref[:, at : at + LANES], nears[r].astype(BF)], axis=1)
        results.append(dot(pair, both, NT).astype(BF))
    for r in range(GROUP):
        at = r * LANES
        out_ref[:, at : at + LANES] = results[r]
        both = jnp.concatenate([diag_ref[at : at + LANES, :], cond_ref[at : at + LANES, :]], axis=1)
        back = dot(results[r], both, NN)
        back_ref[:, at : at + LANES] = back[:, :LANES]
        backs.append(back[:, LANES:])
    terms = [halves(backs[r], backs[r + 1]) for r in range(0, GROUP, 2)]
    fterms_ref[...] = jnp.concatenate([pair[1] for pair in terms], axis=1).astype(BF)
    terms_ref[...] = jnp.concatenate([pair[0] for pair in terms], axis=1).astype(BF)


def block_call(near, fnear, extra, fine_probe, diag, cond, cdiag, ccond):
    pts = fine_probe.shape[1]
    steps = near.shape[0]
    whole = lambda *shape: pl.BlockSpec(shape, lambda g: (0,) * len(shape))
    span = GROUP * LANES
    columns = pl.BlockSpec((64, span), lambda g: (0, g))
    slotted = pl.BlockSpec((None, 64, SLOTS), lambda g: (g, 0, 0))
    rows = pl.BlockSpec((span, LANES), lambda g: (g, 0))
    return pl.pallas_call(
        block_kernel,
        name="blocks",
        grid=(steps,),
        out_shape=(
            jax.ShapeDtypeStruct((64, pts), BF),
            jax.ShapeDtypeStruct((64, pts), F32),
            jax.ShapeDtypeStruct((32, 64), BF),
            jax.ShapeDtypeStruct(near.shape, BF),
            jax.ShapeDtypeStruct(near.shape, BF),
            jax.ShapeDtypeStruct((64, LANES), BF),
            jax.ShapeDtypeStruct((64, LANES), F32),
        ),
        in_specs=[
            slotted, slotted, whole(2, 64, LANES), columns, rows, rows, whole(32, LANES), whole(32, LANES),
        ],
        out_specs=(
            columns, columns, whole(32, 64), slotted, slotted, whole(64, LANES), whole(64, LANES),
        ),
        compiler_params=pltpu.CompilerParams(vmem_limit_bytes=60 * 1024 * 1024),
    )(near, fnear, extra, fine_probe, diag, cond, cdiag, ccond)


def on_device(
    fine_probe, coarse_probe, fine_diag, fine_cond, fine_nbr, coarse_diag, coarse_cond, coarse_nbr
):
    near, fine_near, extra = gather_call(coarse_probe.T, fine_probe, fine_nbr, coarse_nbr)
    fine_out, own_back, coarse_out, terms, fine_terms, extra_terms, extra_own = block_call(
        near, fine_near, extra, fine_probe, fine_diag, fine_cond, coarse_diag, coarse_cond
    )
    coarse_back, fine_back, rim_in = sum_call(
        terms, fine_terms, extra_terms, extra_own, fine_nbr, coarse_nbr, own_back
    )
    last = lax.axis_index("tile") == lax.axis_size("tile") - 1
    rim_in = jnp.where(last, jnp.zeros((), F32), rim_in.astype(F32))
    fine_back = fine_back + jnp.pad(rim_in, ((0, 0), (fine_back.shape[1] - RIM, 0)))
    return fine_out, fine_back, coarse_out.T, coarse_back.T


def solution(mesh):
    columns, rows = P(None, ("grp", "tile")), P(("grp", "tile"), None)
    return jax.shard_map(
        on_device,
        mesh=mesh,
        in_specs=(columns, columns, rows, rows, rows, rows, rows, P()),
        out_specs=(columns, columns, columns, columns),
        check_vma=False,
    )
```

```python
import jax
import jax.numpy as jnp
from jax import lax
from jax.experimental import pallas as pl
from jax.experimental.pallas import tpu as pltpu
from jax.sharding import PartitionSpec as P

RIM = 1024
WIDE = 256
LANES = 128
MESH = pl.DeviceIdType.MESH
NT = (((1,), (1,)), ((), ()))
NN = (((1,), (0,)), ((), ()))
TN = (((0,), (0,)), ((), ()))
BF = jnp.bfloat16
F32 = jnp.float32
GROUP = 16
SLOTS = GROUP * 64
PART = 8


def place():
    grp, tile = lax.axis_index("grp"), lax.axis_index("tile")
    core = tile % 2
    x_hi = (tile // 2) % 2
    y = (tile // 4) % 4
    z = tile // 16
    return grp, z, y, x_hi, core


def dev(grp, z, y, x_hi, core):
    return (grp, ((z * 4 + y) * 2 + x_hi) * 2 + core)


def near_peers(grp, z, y, x_hi, core):
    group = []
    for step in range(1, 8):
        g1, h1, c1 = step // 4, (step // 2) % 2, step % 2
        group.append(((grp + g1) % 2, (x_hi + h1) % 2, (core + c1) % 2))
    return group


def greet(grp, z, y, x_hi, core, others=()):
    barrier = pltpu.get_barrier_semaphore()
    count = 0
    for g1, h1, c1 in near_peers(grp, z, y, x_hi, core):
        pl.semaphore_signal(barrier, inc=1, device_id=dev(g1, z, y, h1, c1), device_id_type=MESH)
        count += 1
    for step in range(1, 8):
        pl.semaphore_signal(
            barrier, inc=1, device_id=dev(grp, (z + step) % 8, y, x_hi, core), device_id_type=MESH
        )
        count += 1
    for step in range(1, 4):
        pl.semaphore_signal(
            barrier, inc=1, device_id=dev(grp, z, (y + step) % 4, x_hi, core), device_id_type=MESH
        )
        count += 1
    for other in others:
        pl.semaphore_signal(barrier, inc=1, device_id=other, device_id_type=MESH)
        count += 1
    return barrier, count


def gather_kernel(
    shard_ref, fine_ref, nbr_ref, clinks_ref, near_ref, fnear_ref, extra_ref,
    got, ctx, held, hots, fhots, acc, xacc,
    s1, r1, s2, r2, s3, r3, s4, r4, s5, r5, s6,
):
    grp, z, y, x_hi, core = place()
    tile = lax.axis_index("tile")
    tiles = lax.axis_size("tile")
    right = (grp, (tile + 1) % tiles)
    left = (grp, (tile + tiles - 1) % tiles)
    spot = grp * 4 + x_hi * 2 + core
    pts = fine_ref.shape[1]
    groups = nbr_ref.shape[0] // GROUP
    load = pltpu.make_async_copy(fine_ref, ctx.at[:, pl.ds(RIM, pts)], s6)
    load.start()
    lane = lax.broadcasted_iota(jnp.int32, (32, LANES), 1) % 32
    tiled = jnp.where(lane == lax.broadcasted_iota(jnp.int32, (32, LANES), 0), jnp.float32(1), jnp.float32(0))
    barrier, count = greet(grp, z, y, x_hi, core, (left, right))
    got[spot] = dot(shard_ref[...], tiled.astype(BF), TN).astype(BF)
    pl.semaphore_wait(barrier, count)
    first = []
    for k, (g1, h1, c1) in enumerate(near_peers(grp, z, y, x_hi, core)):
        part = got.at[spot, pl.ds(pl.multiple_of(c1 * 32, 32), 32), :]
        copy = pltpu.make_async_remote_copy(
            src_ref=part, dst_ref=part, send_sem=s1.at[k], recv_sem=r1.at[k],
            device_id=dev(g1, z, y, h1, c1), device_id_type=MESH,
        )
        copy.start()
        first.append(copy)
    rim = pltpu.make_async_remote_copy(
        src_ref=fine_ref.at[:, pl.ds(pts - RIM, RIM)], dst_ref=ctx.at[:, pl.ds(0, RIM)],
        send_sem=s5, recv_sem=r5, device_id=right, device_id_type=MESH,
    )
    flos, los = [], []
    for g in range(groups):
        lo, hi = fine_slots(nbr_ref, g)
        flos.append(lo)
        fhots[g] = one_hot(hi)
    load.wait()

    def pick_own(g):
        found = jnp.zeros((64, SLOTS), F32)
        for part in range(g + 1):
            found = picked(lane_rows(ctx, 4 + part * PART, PART), fhots[g], flos[g], 4 + part * PART, found)
        fnear_ref[g] = found.astype(BF)

    def pick_rim(g):
        found = picked(lane_rows(ctx, 0, 4), fhots[g], flos[g], 0, fnear_ref[g].astype(F32))
        fnear_ref[g] = found.astype(BF)

    pick_own(0)
    pick_own(1)
    for copy in first:
        copy.wait()
    rows = pl.ds(pl.multiple_of(core * 32, 32), 32)
    lane = lax.broadcasted_iota(jnp.int32, (32, LANES), 1) // 32
    for g in range(2):
        chunk = got[g * 4, rows, :].astype(F32)
        for k in range(1, 4):
            chunk = jnp.where(lane == k, got[g * 4 + k, rows, :].astype(F32), chunk)
        held[z, y, core, :, g * LANES : g * LANES + LANES] = chunk.astype(BF)
    along_z, along_y, swap = {}, {}, {}
    for dz in (1, 7, 2, 6, 3, 5, 4):
        part = held.at[z, y, core]
        along_z[dz] = pltpu.make_async_remote_copy(
            src_ref=part, dst_ref=part, send_sem=s2.at[dz - 1], recv_sem=r2.at[dz - 1],
            device_id=dev(grp, (z + dz) % 8, y, x_hi, core), device_id_type=MESH,
        )
        along_z[dz].start()

    def send_y(dz):
        if dz > 0:
            along_z[dz].wait()
        for k in (1, 0, 2):
            part = held.at[(z + 8 - dz) % 8, y, core]
            copy = pltpu.make_async_remote_copy(
                src_ref=part, dst_ref=part, send_sem=s3.at[dz, k], recv_sem=r3.at[dz, k],
                device_id=dev(grp, z, (y + k + 1) % 4, x_hi, core), device_id_type=MESH,
            )
            copy.start()
            along_y[dz, k] = copy

    def send_swap(dz):
        for k in range(3):
            along_y[dz, k].wait()
        part = held.at[(z + 8 - dz) % 8, :, core]
        swap[dz] = pltpu.make_async_remote_copy(
            src_ref=part, dst_ref=part, send_sem=s4.at[dz], recv_sem=r4.at[dz],
            device_id=dev(grp, z, y, x_hi, 1 - core), device_id_type=MESH,
        )
        swap[dz].start()

    def pick_coarse(pair, start, end):
        origins = [(z + 8 - dz) % 8 for dz in pair]
        for dz in pair:
            swap[dz].wait()
        lhs = jnp.concatenate([held[origin].reshape(WIDE, WIDE) for origin in origins], axis=0)

        def choose(hot, lo, found):
            hits = dot(lhs, hot, NN)
            for j, origin in enumerate(origins):
                for yy in range(4):
                    at = (j * 4 + yy) * 64
                    found = jnp.where(lo == origin * 4 + yy, hits[at : at + 64], found)
            return found

        for g in range(groups):
            found = choose(hots[g], los[g], jnp.zeros((64, SLOTS), F32) if start else acc[g])
            if end:
                near_ref[g] = found.astype(BF)
            else:
                acc[g] = found
        found = choose(xhot, xlo, jnp.zeros((64, LANES), F32) if start else xacc[...])
        if end:
            extra_ref[0] = found.astype(BF)
        else:
            xacc[...] = found

    send_y(0)
    rim.start()
    for g in range(groups):
        lo, hi = coarse_slots(slots(nbr_ref, g, 0))
        los.append(lo)
        hots[g] = one_hot(hi)
    xlo, xhi = coarse_slots(clinks_ref[pl.ds(grp * (tiles // 4) + tile // 4, 1), :])
    xhot = one_hot(xhi)
    send_y(1)
    send_y(7)
    pick_own(2)
    send_y(2)
    send_y(6)
    pick_own(3)
    send_y(3)
    send_y(5)
    send_y(4)
    send_swap(0)
    for g in range(4, groups):
        pick_own(g)
    send_swap(1)
    send_swap(7)
    rim.wait()
    for g in range(groups):
        pick_rim(g)
    send_swap(2)
    send_swap(6)
    pick_coarse((0, 1), True, False)
    send_swap(3)
    send_swap(5)
    send_swap(4)
    pick_coarse((7, 2), False, False)
    pick_coarse((6, 3), False, False)
    pick_coarse((5, 4), False, True)
    own = held[z, y].reshape(64, WIDE)
    extra_ref[1] = jnp.where(grp == 1, own[:, LANES:].astype(F32), own[:, :LANES].astype(F32)).astype(BF)


def gather_call(coarse_shard, fine_probe, nbr, clinks):
    vmem = pl.BlockSpec(memory_space=pltpu.VMEM)
    dma = pltpu.SemaphoreType.DMA
    groups = nbr.shape[0] // GROUP
    near = jax.ShapeDtypeStruct((groups, 64, SLOTS), BF)
    return pl.pallas_call(
        gather_kernel,
        name="coarse_gather",
        out_shape=(near, near, jax.ShapeDtypeStruct((2, 64, LANES), BF)),
        in_specs=[vmem, pl.BlockSpec(memory_space=pl.ANY), vmem, vmem],
        out_specs=(vmem, vmem, vmem),
        scratch_shapes=[
            pltpu.VMEM((8, 64, LANES), BF),
            pltpu.VMEM((64, RIM + fine_probe.shape[1]), BF),
            pltpu.VMEM((8, 4, 2, 32, WIDE), BF),
            pltpu.VMEM((groups, WIDE, SLOTS), BF),
            pltpu.VMEM((groups, WIDE, SLOTS), BF),
            pltpu.VMEM((groups, 64, SLOTS), F32),
            pltpu.VMEM((64, LANES), F32),
            dma((7,)), dma((7,)), dma((7,)), dma((7,)), dma((8, 3)), dma((8, 3)), dma((8,)), dma((8,)),
            dma, dma, dma,
        ],
        compiler_params=pltpu.CompilerParams(
            collective_id=0, has_side_effects=True, vmem_limit_bytes=60 * 1024 * 1024
        ),
    )(coarse_shard, fine_probe, nbr, clinks)


def sum_kernel(
    terms_ref, fterms_ref, extra_ref, xown_ref, nbr_ref, clinks_ref, own_ref, back_ref, fine_ref, rim_in,
    hots, fhots, totals, rim_out, piece, half_out, half_in, acc, y_out, y_in, z_out, z_in, x_out, x_in,
    s1, r1, s2, r2, s3, r3, s4, r4, s5, r5, s6, s7,
):
    grp, z, y, x_hi, core = place()
    tile = lax.axis_index("tile")
    tiles = lax.axis_size("tile")
    right = (grp, (tile + 1) % tiles)
    left = (grp, (tile + tiles - 1) % tiles)
    mine = pl.ds(pl.multiple_of(core * 32, 32), 32)
    other = pl.ds(pl.multiple_of((1 - core) * 32, 32), 32)
    groups = nbr_ref.shape[0] // GROUP
    load = pltpu.make_async_copy(own_ref, totals, s6)
    load.start()
    barrier, count = greet(grp, z, y, x_hi, core, (left, right))
    los, flos = [], []
    for g in range(groups):
        lo, hi = coarse_slots(slots(nbr_ref, g, 0))
        los.append(lo.astype(BF))
        hots[g] = one_hot(hi)
    xlo, xhi = coarse_slots(clinks_ref[pl.ds(grp * (tiles // 4) + tile // 4, 1), :])
    xlo = xlo.astype(BF)
    xhot = one_hot(xhi)
    swap, along_y, along_z = {}, {}, {}

    def spread_coarse(pair):
        targets = [(z + dz) % 8 for dz in pair]

        def lay(terms, lo):
            zero = jnp.zeros_like(terms)
            return jnp.concatenate(
                [jnp.where(lo == (target * 4 + yy).astype(F32).astype(BF), terms, zero)
                 for target in targets for yy in range(4)],
                axis=0,
            )

        total = dot(lay(extra_ref[...], xlo), xhot, NT)
        for g in range(groups):
            total = total + dot(lay(terms_ref[g], los[g]), hots[g], NT)
        for j, dz in enumerate(pair):
            for yy in range(4):
                at = (j * 4 + yy) * 64
                part = total[at : at + 64]
                if dz == 0:
                    own, none = xown_ref[...], jnp.zeros((64, LANES), F32)
                    here = y == yy
                    part = part + jnp.concatenate(
                        [jnp.where(here & (grp == 0), own, none), jnp.where(here & (grp == 1), own, none)], axis=1
                    )
                piece[dz, yy] = part
                half_out[dz, yy] = piece[dz, yy, other, :].astype(BF)

    def send_swap(dz):
        swap[dz] = pltpu.make_async_remote_copy(
            src_ref=half_out.at[dz], dst_ref=half_in.at[dz], send_sem=s1.at[dz], recv_sem=r1.at[dz],
            device_id=dev(grp, z, y, x_hi, 1 - core), device_id_type=MESH,
        )
        swap[dz].start()

    def send_y(dz):
        swap[dz].wait()
        for yy in range(4):
            total = piece[dz, yy, mine, :] + half_in[dz, yy].astype(F32)
            acc[dz, yy] = total
            y_out[dz, yy] = total.astype(BF)
        for k in (1, 0, 2):
            copy = pltpu.make_async_remote_copy(
                src_ref=y_out.at[dz, (y + k + 1) % 4], dst_ref=y_in.at[dz, k],
                send_sem=s2.at[dz, k], recv_sem=r2.at[dz, k],
                device_id=dev(grp, z, (y + k + 1) % 4, x_hi, core), device_id_type=MESH,
            )
            copy.start()
            along_y[dz, k] = copy

    def send_z(dz):
        total = acc[dz, y]
        for k in range(3):
            along_y[dz, k].wait()
            total = total + y_in[dz, k].astype(F32)
        if dz == 0:
            return total
        z_out[dz - 1] = total.astype(BF)
        along_z[dz] = pltpu.make_async_remote_copy(
            src_ref=z_out.at[dz - 1], dst_ref=z_in.at[dz - 1], send_sem=s3.at[dz - 1], recv_sem=r3.at[dz - 1],
            device_id=dev(grp, (z + dz) % 8, y, x_hi, core), device_id_type=MESH,
        )
        along_z[dz].start()

    def spread_sum(first, parts, start):
        total = None
        for g in range(start, groups):
            found = dot(spread(fterms_ref[g], flos[g], first, parts), fhots[g], NT)
            total = found if total is None else total + found
        return total

    stores = []

    def spread_own(part):
        found = spread_sum(4 + part * PART, PART, part)
        for j in range(PART):
            at = (part * PART + j) * WIDE
            totals[:, at : at + WIDE] = totals[:, at : at + WIDE] + found[j * 64 : j * 64 + 64]
        at = pl.ds(part * PART * WIDE, PART * WIDE)
        store = pltpu.make_async_copy(totals.at[:, at], fine_ref.at[:, at], s7.at[part])
        store.start()
        stores.append(store)

    spread_coarse((4, 3))
    pl.semaphore_wait(barrier, count)
    send_swap(4)
    send_swap(3)
    spread_coarse((5, 2))
    send_swap(5)
    send_swap(2)
    send_y(4)
    send_y(3)
    spread_coarse((6, 1))
    send_swap(6)
    send_swap(1)
    send_y(5)
    send_y(2)
    spread_coarse((7, 0))
    send_swap(7)
    send_swap(0)
    send_y(6)
    send_y(1)
    send_z(4)
    send_z(3)
    for g in range(groups):
        lo, hi = fine_slots(nbr_ref, g)
        flos.append(lo.astype(BF))
        fhots[g] = one_hot(hi)
    send_y(7)
    send_y(0)
    send_z(5)
    send_z(2)
    rim_terms = spread_sum(0, 4, 0)
    for j in range(4):
        rim_out[:, j * WIDE : j * WIDE + WIDE] = rim_terms[j * 64 : j * 64 + 64].astype(BF)
    rim = pltpu.make_async_remote_copy(
        src_ref=rim_out, dst_ref=rim_in, send_sem=s5, recv_sem=r5,
        device_id=left, device_id_type=MESH,
    )
    rim.start()
    send_z(6)
    send_z(1)
    load.wait()
    send_z(7)
    total = send_z(0)
    spread_own(0)
    spread_own(1)
    for dz in (4, 3, 5, 2, 6, 1, 7):
        along_z[dz].wait()
        total = total + z_in[dz - 1].astype(F32)
    for g in range(2):
        x_out[g] = total[:, g * LANES : g * LANES + LANES]
    third = []
    spot = grp * 4 + x_hi * 2 + core
    for k, (g1, h1, c1) in enumerate(near_peers(grp, z, y, x_hi, core)):
        copy = pltpu.make_async_remote_copy(
            src_ref=x_out.at[g1], dst_ref=x_in.at[spot], send_sem=s4.at[k], recv_sem=r4.at[k],
            device_id=dev(g1, z, y, h1, c1), device_id_type=MESH,
        )
        copy.start()
        third.append(copy)
    x_in[spot] = x_out[grp]
    for part in range(2, groups):
        spread_own(part)
    rim.wait()
    for copy in third:
        copy.wait()
    which = x_hi * 2 + core
    total = jnp.concatenate(
        [(x_in[half] + x_in[2 + half]) + (x_in[4 + half] + x_in[6 + half]) for half in range(2)], axis=0
    ).T
    part = total[0:32]
    for k in range(1, 4):
        part = jnp.where(which == k, total[k * 32 : k * 32 + 32], part)
    back_ref[...] = part
    for store in stores:
        store.wait()


def sum_call(terms, fterms, xterms, xown, nbr, clinks, own_back):
    vmem = pl.BlockSpec(memory_space=pltpu.VMEM)
    away = pl.BlockSpec(memory_space=pl.ANY)
    dma = pltpu.SemaphoreType.DMA
    groups = nbr.shape[0] // GROUP
    return pl.pallas_call(
        sum_kernel,
        name="coarse_sum",
        out_shape=(
            jax.ShapeDtypeStruct((32, 64), F32),
            jax.ShapeDtypeStruct(own_back.shape, F32),
            jax.ShapeDtypeStruct((64, RIM), BF),
        ),
        in_specs=[vmem] * 6 + [away],
        out_specs=(vmem, away, vmem),
        scratch_shapes=[
            pltpu.VMEM((groups, WIDE, SLOTS), BF),
            pltpu.VMEM((groups, WIDE, SLOTS), BF),
            pltpu.VMEM(own_back.shape, F32),
            pltpu.VMEM((64, RIM), BF),
            pltpu.VMEM((8, 4, 64, WIDE), F32),
            pltpu.VMEM((8, 4, 32, WIDE), BF),
            pltpu.VMEM((8, 4, 32, WIDE), BF),
            pltpu.VMEM((8, 4, 32, WIDE), F32),
            pltpu.VMEM((8, 4, 32, WIDE), BF),
            pltpu.VMEM((8, 3, 32, WIDE), BF),
            pltpu.VMEM((7, 32, WIDE), BF),
            pltpu.VMEM((7, 32, WIDE), BF),
            pltpu.VMEM((2, 32, LANES), F32),
            pltpu.VMEM((8, 32, LANES), F32),
            dma((8,)), dma((8,)), dma((8, 3)), dma((8, 3)), dma((7,)), dma((7,)), dma((7,)), dma((7,)),
            dma, dma, dma, dma((groups,)),
        ],
        compiler_params=pltpu.CompilerParams(
            collective_id=1, has_side_effects=True, vmem_limit_bytes=60 * 1024 * 1024
        ),
    )(terms, fterms, xterms, xown, nbr, clinks, own_back)


def one_hot(hi):
    spots = lax.broadcasted_iota(jnp.int32, (WIDE, hi.shape[1]), 0)
    return jnp.where(spots == hi, jnp.float32(1), jnp.float32(0)).astype(BF)


def dot(a, b, dims):
    return lax.dot_general(a, b, dims, preferred_element_type=F32)


def picked(rows, hot, lo, first, acc):
    found = dot(rows, hot, NN)
    for j in range(found.shape[0] // 64):
        acc = jnp.where(lo == first + j, found[j * 64 : j * 64 + 64], acc)
    return acc


def spread(terms, lo, first, parts):
    zero = jnp.zeros_like(terms)
    return jnp.concatenate([jnp.where(lo == (first + j), terms, zero) for j in range(parts)], axis=0)


def halves(a, b):
    lane = lax.broadcasted_iota(jnp.int32, a.shape, 1)
    low = lane < 64
    return (
        jnp.where(low, a, pltpu.roll(b, 64, 1)),
        jnp.where(low, pltpu.roll(a, 64, 1), b),
    )


def lane_rows(ref, first, parts):
    return jnp.concatenate([ref[:, (first + j) * WIDE : (first + j + 1) * WIDE] for j in range(parts)], axis=0)


def slots(nbr_ref, g, which):
    rows = [nbr_ref[pl.ds(g * GROUP + r, 1), :] for r in range(GROUP)]
    return jnp.concatenate([halves(rows[r], rows[r + 1])[which] for r in range(0, GROUP, 2)], axis=1)


def fine_slots(nbr_ref, g):
    at = slots(nbr_ref, g, 1) - 8192
    return at >> 8, at & 255


def coarse_slots(at):
    lo = jnp.where(at < 0, -1, (at >> 7) & 31)
    return lo, ((at >> 12) << 7) + (at & 127)


def block_kernel(
    near_ref, fnear_ref, extra_ref, fine_ref, diag_ref, cond_ref, cdiag_ref, ccond_ref,
    out_ref, back_ref, cout_ref, terms_ref, fterms_ref, xterms_ref, xown_ref,
):
    g = pl.program_id(0)

    @pl.when(g == 0)
    def _():
        res = dot(cdiag_ref[...], extra_ref[1], NT) + dot(ccond_ref[...], extra_ref[0], NT)
        res = res.astype(BF)
        cout_ref[...] = res
        xown_ref[...] = dot(res, cdiag_ref[...], TN)
        xterms_ref[...] = dot(res, ccond_ref[...], TN).astype(BF)

    nears, results, backs = [], [], []
    for pair in range(GROUP // 2):
        lanes = slice(pair * LANES, pair * LANES + LANES)
        nears.extend(halves(near_ref[:, lanes].astype(F32), fnear_ref[:, lanes].astype(F32)))
    for r in range(GROUP):
        at = r * LANES
        both = jnp.concatenate([diag_ref[at : at + LANES, :], cond_ref[at : at + LANES, :]], axis=1)
        pair = jnp.concatenate([fine_ref[:, at : at + LANES], nears[r].astype(BF)], axis=1)
        results.append(dot(pair, both, NT).astype(BF))
    for r in range(GROUP):
        at = r * LANES
        out_ref[:, at : at + LANES] = results[r]
        both = jnp.concatenate([diag_ref[at : at + LANES, :], cond_ref[at : at + LANES, :]], axis=1)
        back = dot(results[r], both, NN)
        back_ref[:, at : at + LANES] = back[:, :LANES]
        backs.append(back[:, LANES:])
    terms = [halves(backs[r], backs[r + 1]) for r in range(0, GROUP, 2)]
    fterms_ref[...] = jnp.concatenate([pair[1] for pair in terms], axis=1).astype(BF)
    terms_ref[...] = jnp.concatenate([pair[0] for pair in terms], axis=1).astype(BF)


def block_call(near, fnear, extra, fine_probe, diag, cond, cdiag, ccond):
    pts = fine_probe.shape[1]
    steps = near.shape[0]
    whole = lambda *shape: pl.BlockSpec(shape, lambda g: (0,) * len(shape))
    span = GROUP * LANES
    columns = pl.BlockSpec((64, span), lambda g: (0, g))
    slotted = pl.BlockSpec((None, 64, SLOTS), lambda g: (g, 0, 0))
    rows = pl.BlockSpec((span, LANES), lambda g: (g, 0))
    return pl.pallas_call(
        block_kernel,
        name="blocks",
        grid=(steps,),
        out_shape=(
            jax.ShapeDtypeStruct((64, pts), BF),
            jax.ShapeDtypeStruct((64, pts), F32),
            jax.ShapeDtypeStruct((32, 64), BF),
            jax.ShapeDtypeStruct(near.shape, BF),
            jax.ShapeDtypeStruct(near.shape, BF),
            jax.ShapeDtypeStruct((64, LANES), BF),
            jax.ShapeDtypeStruct((64, LANES), F32),
        ),
        in_specs=[
            slotted, slotted, whole(2, 64, LANES), columns, rows, rows, whole(32, LANES), whole(32, LANES),
        ],
        out_specs=(
            columns, columns, whole(32, 64), slotted, slotted, whole(64, LANES), whole(64, LANES),
        ),
        compiler_params=pltpu.CompilerParams(vmem_limit_bytes=60 * 1024 * 1024),
    )(near, fnear, extra, fine_probe, diag, cond, cdiag, ccond)


def finish_kernel(fine_ref, rim_ref, out_ref):
    g = pl.program_id(0)
    out_ref[...] = fine_ref[...]

    @pl.when(g == pl.num_programs(0) - 1)
    def _():
        last = lax.axis_index("tile") == lax.axis_size("tile") - 1
        keep = jnp.where(last, jnp.float32(0), jnp.float32(1))
        out_ref[:, -RIM:] = fine_ref[:, -RIM:] + rim_ref[...].astype(F32) * keep


def finish_call(fine_back, rim):
    columns = pl.BlockSpec((64, GROUP * LANES), lambda g: (0, g))
    return pl.pallas_call(
        finish_kernel,
        name="add_rim",
        grid=(fine_back.shape[1] // (GROUP * LANES),),
        out_shape=jax.ShapeDtypeStruct(fine_back.shape, F32),
        in_specs=[columns, pl.BlockSpec((64, RIM), lambda g: (0, 0))],
        out_specs=columns,
        compiler_params=pltpu.CompilerParams(vmem_limit_bytes=60 * 1024 * 1024),
    )(fine_back, rim)


def on_device(
    fine_probe, coarse_probe, fine_diag, fine_cond, fine_nbr, coarse_diag, coarse_cond, coarse_nbr
):
    near, fine_near, extra = gather_call(coarse_probe.T, fine_probe, fine_nbr, coarse_nbr)
    fine_out, own_back, coarse_out, terms, fine_terms, extra_terms, extra_own = block_call(
        near, fine_near, extra, fine_probe, fine_diag, fine_cond, coarse_diag, coarse_cond
    )
    coarse_back, fine_back, rim_in = sum_call(
        terms, fine_terms, extra_terms, extra_own, fine_nbr, coarse_nbr, own_back
    )
    fine_back = finish_call(fine_back, rim_in)
    return fine_out, fine_back, coarse_out.T, coarse_back.T


def solution(mesh):
    columns, rows = P(None, ("grp", "tile")), P(("grp", "tile"), None)
    return jax.shard_map(
        on_device,
        mesh=mesh,
        in_specs=(columns, columns, rows, rows, rows, rows, rows, P()),
        out_specs=(columns, columns, columns, columns),
        check_vma=False,
    )
```

```python
import jax
import jax.numpy as jnp
from jax import lax
from jax.experimental import pallas as pl
from jax.experimental.pallas import tpu as pltpu
from jax.sharding import PartitionSpec as P

RIM = 1024
WIDE = 256
LANES = 128
MESH = pl.DeviceIdType.MESH
NT = (((1,), (1,)), ((), ()))
NN = (((1,), (0,)), ((), ()))
TN = (((0,), (0,)), ((), ()))
BF = jnp.bfloat16
F32 = jnp.float32
GROUP = 16
SLOTS = GROUP * 64
PART = 8


def place():
    grp, tile = lax.axis_index("grp"), lax.axis_index("tile")
    core = tile % 2
    x_hi = (tile // 2) % 2
    y = (tile // 4) % 4
    z = tile // 16
    return grp, z, y, x_hi, core


def dev(grp, z, y, x_hi, core):
    return (grp, ((z * 4 + y) * 2 + x_hi) * 2 + core)


def near_peers(grp, z, y, x_hi, core):
    group = []
    for step in range(1, 8):
        g1, h1, c1 = step // 4, (step // 2) % 2, step % 2
        group.append(((grp + g1) % 2, (x_hi + h1) % 2, (core + c1) % 2))
    return group


def greet(grp, z, y, x_hi, core, others=()):
    barrier = pltpu.get_barrier_semaphore()
    count = 0
    for g1, h1, c1 in near_peers(grp, z, y, x_hi, core):
        pl.semaphore_signal(barrier, inc=1, device_id=dev(g1, z, y, h1, c1), device_id_type=MESH)
        count += 1
    for step in range(1, 8):
        pl.semaphore_signal(
            barrier, inc=1, device_id=dev(grp, (z + step) % 8, y, x_hi, core), device_id_type=MESH
        )
        count += 1
    for step in range(1, 4):
        pl.semaphore_signal(
            barrier, inc=1, device_id=dev(grp, z, (y + step) % 4, x_hi, core), device_id_type=MESH
        )
        count += 1
    for other in others:
        pl.semaphore_signal(barrier, inc=1, device_id=other, device_id_type=MESH)
        count += 1
    return barrier, count


def gather_kernel(
    shard_ref, fine_ref, nbr_ref, clinks_ref, near_ref, fnear_ref, extra_ref,
    got, ctx, held, hots, fhots, acc, xacc,
    s1, r1, s2, r2, s3, r3, s4, r4, s5, r5, s6,
):
    grp, z, y, x_hi, core = place()
    tile = lax.axis_index("tile")
    tiles = lax.axis_size("tile")
    right = (grp, (tile + 1) % tiles)
    left = (grp, (tile + tiles - 1) % tiles)
    spot = grp * 4 + x_hi * 2 + core
    pts = fine_ref.shape[1]
    groups = nbr_ref.shape[0] // GROUP
    load = pltpu.make_async_copy(fine_ref, ctx.at[:, pl.ds(RIM, pts)], s6)
    load.start()
    lane = lax.broadcasted_iota(jnp.int32, (32, LANES), 1) % 32
    tiled = jnp.where(lane == lax.broadcasted_iota(jnp.int32, (32, LANES), 0), jnp.float32(1), jnp.float32(0))
    barrier, count = greet(grp, z, y, x_hi, core, (left, right))
    got[spot] = dot(shard_ref[...], tiled.astype(BF), TN).astype(BF)
    pl.semaphore_wait(barrier, count)
    first = []
    for k, (g1, h1, c1) in enumerate(near_peers(grp, z, y, x_hi, core)):
        part = got.at[spot, pl.ds(pl.multiple_of(c1 * 32, 32), 32), :]
        copy = pltpu.make_async_remote_copy(
            src_ref=part, dst_ref=part, send_sem=s1.at[k], recv_sem=r1.at[k],
            device_id=dev(g1, z, y, h1, c1), device_id_type=MESH,
        )
        copy.start()
        first.append(copy)
    rim = pltpu.make_async_remote_copy(
        src_ref=fine_ref.at[:, pl.ds(pts - RIM, RIM)], dst_ref=ctx.at[:, pl.ds(0, RIM)],
        send_sem=s5, recv_sem=r5, device_id=right, device_id_type=MESH,
    )
    flos, los = [], []
    for g in range(groups):
        lo, hi = fine_slots(nbr_ref, g)
        flos.append(lo)
        fhots[g] = one_hot(hi)
    load.wait()

    def pick_own(g):
        found = jnp.zeros((64, SLOTS), F32)
        for part in range(g + 1):
            found = picked(lane_rows(ctx, 4 + part * PART, PART), fhots[g], flos[g], 4 + part * PART, found)
        fnear_ref[g] = found.astype(BF)

    def pick_rim(g):
        found = picked(lane_rows(ctx, 0, 4), fhots[g], flos[g], 0, fnear_ref[g].astype(F32))
        fnear_ref[g] = found.astype(BF)

    pick_own(0)
    pick_own(1)
    for copy in first:
        copy.wait()
    rows = pl.ds(pl.multiple_of(core * 32, 32), 32)
    lane = lax.broadcasted_iota(jnp.int32, (32, LANES), 1) // 32
    for g in range(2):
        chunk = got[g * 4, rows, :].astype(F32)
        for k in range(1, 4):
            chunk = jnp.where(lane == k, got[g * 4 + k, rows, :].astype(F32), chunk)
        held[z, y, core, :, g * LANES : g * LANES + LANES] = chunk.astype(BF)
    along_z, along_y, swap = {}, {}, {}
    for dz in (1, 7, 2, 6, 3, 5, 4):
        part = held.at[z, y, core]
        along_z[dz] = pltpu.make_async_remote_copy(
            src_ref=part, dst_ref=part, send_sem=s2.at[dz - 1], recv_sem=r2.at[dz - 1],
            device_id=dev(grp, (z + dz) % 8, y, x_hi, core), device_id_type=MESH,
        )
        along_z[dz].start()

    def send_y(dz):
        if dz > 0:
            along_z[dz].wait()
        for k in (1, 0, 2):
            part = held.at[(z + 8 - dz) % 8, y, core]
            copy = pltpu.make_async_remote_copy(
                src_ref=part, dst_ref=part, send_sem=s3.at[dz, k], recv_sem=r3.at[dz, k],
                device_id=dev(grp, z, (y + k + 1) % 4, x_hi, core), device_id_type=MESH,
            )
            copy.start()
            along_y[dz, k] = copy

    def send_swap(dz):
        for k in range(3):
            along_y[dz, k].wait()
        part = held.at[(z + 8 - dz) % 8, :, core]
        swap[dz] = pltpu.make_async_remote_copy(
            src_ref=part, dst_ref=part, send_sem=s4.at[dz], recv_sem=r4.at[dz],
            device_id=dev(grp, z, y, x_hi, 1 - core), device_id_type=MESH,
        )
        swap[dz].start()

    def pick_coarse(pair, start, end):
        origins = [(z + 8 - dz) % 8 for dz in pair]
        for dz in pair:
            swap[dz].wait()
        lhs = jnp.concatenate([held[origin].reshape(WIDE, WIDE) for origin in origins], axis=0)

        def choose(hot, lo, found):
            hits = dot(lhs, hot, NN)
            for j, origin in enumerate(origins):
                for yy in range(4):
                    at = (j * 4 + yy) * 64
                    found = jnp.where(lo == origin * 4 + yy, hits[at : at + 64], found)
            return found

        for g in range(groups):
            found = choose(hots[g], los[g], jnp.zeros((64, SLOTS), F32) if start else acc[g])
            if end:
                near_ref[g] = found.astype(BF)
            else:
                acc[g] = found
        found = choose(xhot, xlo, jnp.zeros((64, LANES), F32) if start else xacc[...])
        if end:
            extra_ref[0] = found.astype(BF)
        else:
            xacc[...] = found

    send_y(0)
    rim.start()
    for g in range(groups):
        lo, hi = coarse_slots(slots(nbr_ref, g, 0))
        los.append(lo)
        hots[g] = one_hot(hi)
    xlo, xhi = coarse_slots(clinks_ref[pl.ds(grp * (tiles // 4) + tile // 4, 1), :])
    xhot = one_hot(xhi)
    send_y(1)
    send_y(7)
    pick_own(2)
    send_y(2)
    send_y(6)
    pick_own(3)
    send_y(3)
    send_y(5)
    send_y(4)
    send_swap(0)
    for g in range(4, groups):
        pick_own(g)
    send_swap(1)
    send_swap(7)
    rim.wait()
    for g in range(groups):
        pick_rim(g)
    send_swap(2)
    send_swap(6)
    pick_coarse((0, 1), True, False)
    send_swap(3)
    send_swap(5)
    send_swap(4)
    pick_coarse((7, 2), False, False)
    pick_coarse((6, 3), False, False)
    pick_coarse((5, 4), False, True)
    own = held[z, y].reshape(64, WIDE)
    extra_ref[1] = jnp.where(grp == 1, own[:, LANES:].astype(F32), own[:, :LANES].astype(F32)).astype(BF)


def gather_call(coarse_shard, fine_probe, nbr, clinks):
    vmem = pl.BlockSpec(memory_space=pltpu.VMEM)
    dma = pltpu.SemaphoreType.DMA
    groups = nbr.shape[0] // GROUP
    near = jax.ShapeDtypeStruct((groups, 64, SLOTS), BF)
    return pl.pallas_call(
        gather_kernel,
        name="coarse_gather",
        out_shape=(near, near, jax.ShapeDtypeStruct((2, 64, LANES), BF)),
        in_specs=[vmem, pl.BlockSpec(memory_space=pl.ANY), vmem, vmem],
        out_specs=(vmem, vmem, vmem),
        scratch_shapes=[
            pltpu.VMEM((8, 64, LANES), BF),
            pltpu.VMEM((64, RIM + fine_probe.shape[1]), BF),
            pltpu.VMEM((8, 4, 2, 32, WIDE), BF),
            pltpu.VMEM((groups, WIDE, SLOTS), BF),
            pltpu.VMEM((groups, WIDE, SLOTS), BF),
            pltpu.VMEM((groups, 64, SLOTS), F32),
            pltpu.VMEM((64, LANES), F32),
            dma((7,)), dma((7,)), dma((7,)), dma((7,)), dma((8, 3)), dma((8, 3)), dma((8,)), dma((8,)),
            dma, dma, dma,
        ],
        compiler_params=pltpu.CompilerParams(
            collective_id=0, has_side_effects=True, vmem_limit_bytes=60 * 1024 * 1024
        ),
    )(coarse_shard, fine_probe, nbr, clinks)


def sum_kernel(
    terms_ref, extra_ref, xown_ref, nbr_ref, clinks_ref, rim_out, back_ref, rim_in,
    hots, piece, half_out, half_in, acc, y_out, y_in, z_out, z_in, x_out, x_in,
    s1, r1, s2, r2, s3, r3, s4, r4, s5, r5,
):
    grp, z, y, x_hi, core = place()
    tile = lax.axis_index("tile")
    tiles = lax.axis_size("tile")
    right = (grp, (tile + 1) % tiles)
    left = (grp, (tile + tiles - 1) % tiles)
    mine = pl.ds(pl.multiple_of(core * 32, 32), 32)
    other = pl.ds(pl.multiple_of((1 - core) * 32, 32), 32)
    groups = nbr_ref.shape[0] // GROUP
    barrier, count = greet(grp, z, y, x_hi, core, (left, right))
    los = []
    for g in range(groups):
        lo, hi = coarse_slots(slots(nbr_ref, g, 0))
        los.append(lo.astype(BF))
        hots[g] = one_hot(hi)
    xlo, xhi = coarse_slots(clinks_ref[pl.ds(grp * (tiles // 4) + tile // 4, 1), :])
    xlo = xlo.astype(BF)
    xhot = one_hot(xhi)
    swap, along_y, along_z = {}, {}, {}

    def spread_coarse(pair):
        targets = [(z + dz) % 8 for dz in pair]

        def lay(terms, lo):
            zero = jnp.zeros_like(terms)
            return jnp.concatenate(
                [jnp.where(lo == (target * 4 + yy).astype(F32).astype(BF), terms, zero)
                 for target in targets for yy in range(4)],
                axis=0,
            )

        total = dot(lay(extra_ref[...], xlo), xhot, NT)
        for g in range(groups):
            total = total + dot(lay(terms_ref[g], los[g]), hots[g], NT)
        for j, dz in enumerate(pair):
            for yy in range(4):
                at = (j * 4 + yy) * 64
                part = total[at : at + 64]
                if dz == 0:
                    own, none = xown_ref[...], jnp.zeros((64, LANES), F32)
                    here = y == yy
                    part = part + jnp.concatenate(
                        [jnp.where(here & (grp == 0), own, none), jnp.where(here & (grp == 1), own, none)], axis=1
                    )
                piece[dz, yy] = part
                half_out[dz, yy] = piece[dz, yy, other, :].astype(BF)

    def send_swap(dz):
        swap[dz] = pltpu.make_async_remote_copy(
            src_ref=half_out.at[dz], dst_ref=half_in.at[dz], send_sem=s1.at[dz], recv_sem=r1.at[dz],
            device_id=dev(grp, z, y, x_hi, 1 - core), device_id_type=MESH,
        )
        swap[dz].start()

    def send_y(dz):
        swap[dz].wait()
        for yy in range(4):
            total = piece[dz, yy, mine, :] + half_in[dz, yy].astype(F32)
            acc[dz, yy] = total
            y_out[dz, yy] = total.astype(BF)
        for k in (1, 0, 2):
            copy = pltpu.make_async_remote_copy(
                src_ref=y_out.at[dz, (y + k + 1) % 4], dst_ref=y_in.at[dz, k],
                send_sem=s2.at[dz, k], recv_sem=r2.at[dz, k],
                device_id=dev(grp, z, (y + k + 1) % 4, x_hi, core), device_id_type=MESH,
            )
            copy.start()
            along_y[dz, k] = copy

    def send_z(dz):
        total = acc[dz, y]
        for k in range(3):
            along_y[dz, k].wait()
            total = total + y_in[dz, k].astype(F32)
        if dz == 0:
            return total
        z_out[dz - 1] = total.astype(BF)
        along_z[dz] = pltpu.make_async_remote_copy(
            src_ref=z_out.at[dz - 1], dst_ref=z_in.at[dz - 1], send_sem=s3.at[dz - 1], recv_sem=r3.at[dz - 1],
            device_id=dev(grp, (z + dz) % 8, y, x_hi, core), device_id_type=MESH,
        )
        along_z[dz].start()

    spread_coarse((4, 3))
    pl.semaphore_wait(barrier, count)
    rim = pltpu.make_async_remote_copy(
        src_ref=rim_out, dst_ref=rim_in, send_sem=s5, recv_sem=r5,
        device_id=left, device_id_type=MESH,
    )
    send_swap(4)
    send_swap(3)
    spread_coarse((5, 2))
    send_swap(5)
    send_swap(2)
    send_y(4)
    send_y(3)
    spread_coarse((6, 1))
    send_swap(6)
    send_swap(1)
    send_y(5)
    send_y(2)
    spread_coarse((7, 0))
    send_swap(7)
    send_swap(0)
    send_y(6)
    send_y(1)
    send_z(4)
    send_z(3)
    rim.start()
    send_y(7)
    send_y(0)
    send_z(5)
    send_z(2)
    send_z(6)
    send_z(1)
    send_z(7)
    total = send_z(0)
    for dz in (4, 3, 5, 2, 6, 1, 7):
        along_z[dz].wait()
        total = total + z_in[dz - 1].astype(F32)
    for g in range(2):
        x_out[g] = total[:, g * LANES : g * LANES + LANES]
    third = []
    spot = grp * 4 + x_hi * 2 + core
    for k, (g1, h1, c1) in enumerate(near_peers(grp, z, y, x_hi, core)):
        copy = pltpu.make_async_remote_copy(
            src_ref=x_out.at[g1], dst_ref=x_in.at[spot], send_sem=s4.at[k], recv_sem=r4.at[k],
            device_id=dev(g1, z, y, h1, c1), device_id_type=MESH,
        )
        copy.start()
        third.append(copy)
    x_in[spot] = x_out[grp]
    rim.wait()
    for copy in third:
        copy.wait()
    which = x_hi * 2 + core
    total = jnp.concatenate(
        [(x_in[half] + x_in[2 + half]) + (x_in[4 + half] + x_in[6 + half]) for half in range(2)], axis=0
    ).T
    part = total[0:32]
    for k in range(1, 4):
        part = jnp.where(which == k, total[k * 32 : k * 32 + 32], part)
    back_ref[...] = part


def sum_call(terms, xterms, xown, nbr, clinks, rim_terms):
    vmem = pl.BlockSpec(memory_space=pltpu.VMEM)
    dma = pltpu.SemaphoreType.DMA
    groups = nbr.shape[0] // GROUP
    return pl.pallas_call(
        sum_kernel,
        name="coarse_sum",
        out_shape=(
            jax.ShapeDtypeStruct((32, 64), F32),
            jax.ShapeDtypeStruct((64, RIM), BF),
        ),
        in_specs=[vmem] * 6,
        out_specs=(vmem, vmem),
        scratch_shapes=[
            pltpu.VMEM((groups, WIDE, SLOTS), BF),
            pltpu.VMEM((8, 4, 64, WIDE), F32),
            pltpu.VMEM((8, 4, 32, WIDE), BF),
            pltpu.VMEM((8, 4, 32, WIDE), BF),
            pltpu.VMEM((8, 4, 32, WIDE), F32),
            pltpu.VMEM((8, 4, 32, WIDE), BF),
            pltpu.VMEM((8, 3, 32, WIDE), BF),
            pltpu.VMEM((7, 32, WIDE), BF),
            pltpu.VMEM((7, 32, WIDE), BF),
            pltpu.VMEM((2, 32, LANES), F32),
            pltpu.VMEM((8, 32, LANES), F32),
            dma((8,)), dma((8,)), dma((8, 3)), dma((8, 3)), dma((7,)), dma((7,)), dma((7,)), dma((7,)),
            dma, dma,
        ],
        compiler_params=pltpu.CompilerParams(
            collective_id=1, has_side_effects=True, vmem_limit_bytes=60 * 1024 * 1024
        ),
    )(terms, xterms, xown, nbr, clinks, rim_terms)


def one_hot(hi):
    spots = lax.broadcasted_iota(jnp.int32, (WIDE, hi.shape[1]), 0)
    return jnp.where(spots == hi, jnp.float32(1), jnp.float32(0)).astype(BF)


def dot(a, b, dims):
    return lax.dot_general(a, b, dims, preferred_element_type=F32)


def picked(rows, hot, lo, first, acc):
    found = dot(rows, hot, NN)
    for j in range(found.shape[0] // 64):
        acc = jnp.where(lo == first + j, found[j * 64 : j * 64 + 64], acc)
    return acc


def spread(terms, lo, first, parts):
    zero = jnp.zeros_like(terms)
    return jnp.concatenate([jnp.where(lo == (first + j), terms, zero) for j in range(parts)], axis=0)


def halves(a, b):
    lane = lax.broadcasted_iota(jnp.int32, a.shape, 1)
    low = lane < 64
    return (
        jnp.where(low, a, pltpu.roll(b, 64, 1)),
        jnp.where(low, pltpu.roll(a, 64, 1), b),
    )


def lane_rows(ref, first, parts):
    return jnp.concatenate([ref[:, (first + j) * WIDE : (first + j + 1) * WIDE] for j in range(parts)], axis=0)


def slots(nbr_ref, g, which):
    rows = [nbr_ref[pl.ds(g * GROUP + r, 1), :] for r in range(GROUP)]
    return jnp.concatenate([halves(rows[r], rows[r + 1])[which] for r in range(0, GROUP, 2)], axis=1)


def fine_slots(nbr_ref, g):
    at = slots(nbr_ref, g, 1) - 8192
    return at >> 8, at & 255


def coarse_slots(at):
    lo = jnp.where(at < 0, -1, (at >> 7) & 31)
    return lo, ((at >> 12) << 7) + (at & 127)


def block_kernel(
    near_ref, fnear_ref, extra_ref, fine_ref, nbr_ref, diag_ref, cond_ref, cdiag_ref, ccond_ref,
    out_ref, back_ref, cout_ref, terms_ref, xterms_ref, xown_ref, rim_ref,
    totals,
):
    steps = pl.num_programs(0)
    g = steps - 1 - pl.program_id(0)

    @pl.when(g == steps - 1)
    def _():
        totals[...] = jnp.zeros_like(totals)
        res = dot(cdiag_ref[...], extra_ref[1], NT) + dot(ccond_ref[...], extra_ref[0], NT)
        res = res.astype(BF)
        cout_ref[...] = res
        xown_ref[...] = dot(res, cdiag_ref[...], TN)
        xterms_ref[...] = dot(res, ccond_ref[...], TN).astype(BF)

    lo, hi = fine_slots(nbr_ref, g)
    lo, hot = lo.astype(BF), one_hot(hi)
    nears, results, backs, own_back = [], [], [], []
    for pair in range(GROUP // 2):
        lanes = slice(pair * LANES, pair * LANES + LANES)
        nears.extend(halves(near_ref[:, lanes].astype(F32), fnear_ref[:, lanes].astype(F32)))
    for r in range(GROUP):
        at = r * LANES
        both = jnp.concatenate([diag_ref[at : at + LANES, :], cond_ref[at : at + LANES, :]], axis=1)
        pair = jnp.concatenate([fine_ref[:, at : at + LANES], nears[r].astype(BF)], axis=1)
        results.append(dot(pair, both, NT).astype(BF))
    for r in range(GROUP):
        at = r * LANES
        out_ref[:, at : at + LANES] = results[r]
        both = jnp.concatenate([diag_ref[at : at + LANES, :], cond_ref[at : at + LANES, :]], axis=1)
        back = dot(results[r], both, NN)
        own_back.append(back[:, :LANES])
        backs.append(back[:, LANES:])
    terms = [halves(backs[r], backs[r + 1]) for r in range(0, GROUP, 2)]
    terms_ref[...] = jnp.concatenate([pair[0] for pair in terms], axis=1).astype(BF)
    fterms = jnp.concatenate([pair[1] for pair in terms], axis=1).astype(BF)

    def add(first, parts):
        found = dot(spread(fterms, lo, first, parts), hot, NT)
        for j in range(parts):
            at = slice((first + j) * WIDE, (first + j + 1) * WIDE)
            totals[:, at] = totals[:, at] + found[j * 64 : j * 64 + 64]

    add(0, 4)
    for section in range((totals.shape[1] - RIM) // (PART * WIDE)):

        @pl.when(section <= g)
        def _():
            add(4 + section * PART, PART)

    span = PART * WIDE
    mine = pl.ds(pl.multiple_of(RIM + g * span, RIM), span)
    back_ref[...] = totals[:, mine] + jnp.concatenate(own_back, axis=1)

    @pl.when(g == 0)
    def _():
        rim_ref[...] = totals[:, 0:RIM].astype(BF)


def block_call(near, fnear, extra, fine_probe, nbr, diag, cond, cdiag, ccond):
    pts = fine_probe.shape[1]
    steps = near.shape[0]
    whole = lambda *shape: pl.BlockSpec(shape, lambda g: (0,) * len(shape))
    span = GROUP * LANES
    columns = pl.BlockSpec((64, span), lambda g: (0, steps - 1 - g))
    slotted = pl.BlockSpec((None, 64, SLOTS), lambda g: (steps - 1 - g, 0, 0))
    rows = pl.BlockSpec((span, LANES), lambda g: (steps - 1 - g, 0))
    return pl.pallas_call(
        block_kernel,
        name="blocks",
        grid=(steps,),
        out_shape=(
            jax.ShapeDtypeStruct((64, pts), BF),
            jax.ShapeDtypeStruct((64, pts), F32),
            jax.ShapeDtypeStruct((32, 64), BF),
            jax.ShapeDtypeStruct(near.shape, BF),
            jax.ShapeDtypeStruct((64, LANES), BF),
            jax.ShapeDtypeStruct((64, LANES), F32),
            jax.ShapeDtypeStruct((64, RIM), BF),
        ),
        in_specs=[
            slotted, slotted, whole(2, 64, LANES), columns, whole(*nbr.shape), rows, rows,
            whole(32, LANES), whole(32, LANES),
        ],
        out_specs=(
            columns, columns, whole(32, 64), slotted, whole(64, LANES), whole(64, LANES), whole(64, RIM),
        ),
        scratch_shapes=[pltpu.VMEM((64, RIM + pts), F32)],
        compiler_params=pltpu.CompilerParams(vmem_limit_bytes=60 * 1024 * 1024),
    )(near, fnear, extra, fine_probe, nbr, diag, cond, cdiag, ccond)


def finish_kernel(fine_ref, rim_ref, out_ref):
    last = lax.axis_index("tile") == lax.axis_size("tile") - 1
    keep = jnp.where(last, jnp.float32(0), jnp.float32(1))
    out_ref[...] = fine_ref[...] + rim_ref[...].astype(F32) * keep


def finish_call(fine_back, rim):
    final = fine_back.shape[1] // RIM - 1
    columns = pl.BlockSpec((64, RIM), lambda g: (0, final))
    return pl.pallas_call(
        finish_kernel,
        name="add_rim",
        grid=(1,),
        out_shape=jax.ShapeDtypeStruct(fine_back.shape, F32),
        in_specs=[columns, pl.BlockSpec((64, RIM), lambda g: (0, 0))],
        out_specs=columns,
        input_output_aliases={0: 0},
        compiler_params=pltpu.CompilerParams(vmem_limit_bytes=60 * 1024 * 1024),
    )(fine_back, rim)


def on_device(
    fine_probe, coarse_probe, fine_diag, fine_cond, fine_nbr, coarse_diag, coarse_cond, coarse_nbr
):
    near, fine_near, extra = gather_call(coarse_probe.T, fine_probe, fine_nbr, coarse_nbr)
    fine_out, fine_back, coarse_out, terms, extra_terms, extra_own, rim_terms = block_call(
        near, fine_near, extra, fine_probe, fine_nbr, fine_diag, fine_cond, coarse_diag, coarse_cond
    )
    coarse_back, rim_in = sum_call(terms, extra_terms, extra_own, fine_nbr, coarse_nbr, rim_terms)
    fine_back = finish_call(fine_back, rim_in)
    return fine_out, fine_back, coarse_out.T, coarse_back.T


def solution(mesh):
    columns, rows = P(None, ("grp", "tile")), P(("grp", "tile"), None)
    return jax.shard_map(
        on_device,
        mesh=mesh,
        in_specs=(columns, columns, rows, rows, rows, rows, rows, P()),
        out_specs=(columns, columns, columns, columns),
        check_vma=False,
    )
```

```python
import jax
import jax.numpy as jnp
from jax import lax
from jax.experimental import pallas as pl
from jax.experimental.pallas import tpu as pltpu
from jax.sharding import PartitionSpec as P

RIM = 1024
WIDE = 256
LANES = 128
MESH = pl.DeviceIdType.MESH
NT = (((1,), (1,)), ((), ()))
NN = (((1,), (0,)), ((), ()))
TN = (((0,), (0,)), ((), ()))
BF = jnp.bfloat16
F32 = jnp.float32
GROUP = 16
SLOTS = GROUP * 64
PART = 8


def place():
    grp, tile = lax.axis_index("grp"), lax.axis_index("tile")
    core = tile % 2
    x_hi = (tile // 2) % 2
    y = (tile // 4) % 4
    z = tile // 16
    return grp, z, y, x_hi, core


def dev(grp, z, y, x_hi, core):
    return (grp, ((z * 4 + y) * 2 + x_hi) * 2 + core)


def near_peers(grp, z, y, x_hi, core):
    group = []
    for step in range(1, 8):
        g1, h1, c1 = step // 4, (step // 2) % 2, step % 2
        group.append(((grp + g1) % 2, (x_hi + h1) % 2, (core + c1) % 2))
    return group


def greet(grp, z, y, x_hi, core, others=()):
    barrier = pltpu.get_barrier_semaphore()
    count = 0
    for g1, h1, c1 in near_peers(grp, z, y, x_hi, core):
        pl.semaphore_signal(barrier, inc=1, device_id=dev(g1, z, y, h1, c1), device_id_type=MESH)
        count += 1
    for step in range(1, 8):
        pl.semaphore_signal(
            barrier, inc=1, device_id=dev(grp, (z + step) % 8, y, x_hi, core), device_id_type=MESH
        )
        count += 1
    for step in range(1, 4):
        pl.semaphore_signal(
            barrier, inc=1, device_id=dev(grp, z, (y + step) % 4, x_hi, core), device_id_type=MESH
        )
        count += 1
    for other in others:
        pl.semaphore_signal(barrier, inc=1, device_id=other, device_id_type=MESH)
        count += 1
    return barrier, count


def gather_kernel(
    shard_ref, fine_ref, nbr_ref, clinks_ref, near_ref, fnear_ref, extra_ref,
    got, ctx, held, hots, fhots, acc, xacc,
    s1, r1, s2, r2, s3, r3, s4, r4, s5, r5, s6,
):
    grp, z, y, x_hi, core = place()
    tile = lax.axis_index("tile")
    tiles = lax.axis_size("tile")
    right = (grp, (tile + 1) % tiles)
    left = (grp, (tile + tiles - 1) % tiles)
    spot = grp * 4 + x_hi * 2 + core
    pts = fine_ref.shape[1]
    groups = nbr_ref.shape[0] // GROUP
    load = pltpu.make_async_copy(fine_ref, ctx.at[:, pl.ds(RIM, pts)], s6)
    load.start()
    lane = lax.broadcasted_iota(jnp.int32, (32, LANES), 1) % 32
    tiled = jnp.where(lane == lax.broadcasted_iota(jnp.int32, (32, LANES), 0), jnp.float32(1), jnp.float32(0))
    barrier, count = greet(grp, z, y, x_hi, core, (left, right))
    got[spot] = dot(shard_ref[...], tiled.astype(BF), TN).astype(BF)
    pl.semaphore_wait(barrier, count)
    first = []
    for k, (g1, h1, c1) in enumerate(near_peers(grp, z, y, x_hi, core)):
        part = got.at[spot, pl.ds(pl.multiple_of(c1 * 32, 32), 32), :]
        copy = pltpu.make_async_remote_copy(
            src_ref=part, dst_ref=part, send_sem=s1.at[k], recv_sem=r1.at[k],
            device_id=dev(g1, z, y, h1, c1), device_id_type=MESH,
        )
        copy.start()
        first.append(copy)
    rim = pltpu.make_async_remote_copy(
        src_ref=fine_ref.at[:, pl.ds(pts - RIM, RIM)], dst_ref=ctx.at[:, pl.ds(0, RIM)],
        send_sem=s5, recv_sem=r5, device_id=right, device_id_type=MESH,
    )
    flos, los = [], []
    for g in range(groups):
        lo, hi = fine_slots(nbr_ref, g)
        flos.append(lo)
        fhots[g] = one_hot(hi)
    load.wait()

    def pick_own(g):
        found = jnp.zeros((64, SLOTS), F32)
        for part in range(g + 1):
            found = picked(lane_rows(ctx, 4 + part * PART, PART), fhots[g], flos[g], 4 + part * PART, found)
        fnear_ref[g] = found.astype(BF)

    def pick_rim(g):
        found = picked(lane_rows(ctx, 0, 4), fhots[g], flos[g], 0, fnear_ref[g].astype(F32))
        fnear_ref[g] = found.astype(BF)

    pick_own(0)
    pick_own(1)
    for copy in first:
        copy.wait()
    rows = pl.ds(pl.multiple_of(core * 32, 32), 32)
    lane = lax.broadcasted_iota(jnp.int32, (32, LANES), 1) // 32
    for g in range(2):
        chunk = got[g * 4, rows, :].astype(F32)
        for k in range(1, 4):
            chunk = jnp.where(lane == k, got[g * 4 + k, rows, :].astype(F32), chunk)
        held[z, y, core, :, g * LANES : g * LANES + LANES] = chunk.astype(BF)
    along_z, along_y, swap = {}, {}, {}
    for dz in (1, 7, 2, 6, 3, 5, 4):
        part = held.at[z, y, core]
        along_z[dz] = pltpu.make_async_remote_copy(
            src_ref=part, dst_ref=part, send_sem=s2.at[dz - 1], recv_sem=r2.at[dz - 1],
            device_id=dev(grp, (z + dz) % 8, y, x_hi, core), device_id_type=MESH,
        )
        along_z[dz].start()

    def send_y(dz):
        if dz > 0:
            along_z[dz].wait()
        for k in (1, 0, 2):
            part = held.at[(z + 8 - dz) % 8, y, core]
            copy = pltpu.make_async_remote_copy(
                src_ref=part, dst_ref=part, send_sem=s3.at[dz, k], recv_sem=r3.at[dz, k],
                device_id=dev(grp, z, (y + k + 1) % 4, x_hi, core), device_id_type=MESH,
            )
            copy.start()
            along_y[dz, k] = copy

    def send_swap(dz):
        for k in range(3):
            along_y[dz, k].wait()
        part = held.at[(z + 8 - dz) % 8, :, core]
        swap[dz] = pltpu.make_async_remote_copy(
            src_ref=part, dst_ref=part, send_sem=s4.at[dz], recv_sem=r4.at[dz],
            device_id=dev(grp, z, y, x_hi, 1 - core), device_id_type=MESH,
        )
        swap[dz].start()

    def pick_coarse(pair, start, end):
        origins = [(z + 8 - dz) % 8 for dz in pair]
        for dz in pair:
            swap[dz].wait()
        lhs = jnp.concatenate([held[origin].reshape(WIDE, WIDE) for origin in origins], axis=0)

        def choose(hot, lo, found):
            hits = dot(lhs, hot, NN)
            for j, origin in enumerate(origins):
                for yy in range(4):
                    at = (j * 4 + yy) * 64
                    found = jnp.where(lo == origin * 4 + yy, hits[at : at + 64], found)
            return found

        for g in range(groups):
            found = choose(hots[g], los[g], jnp.zeros((64, SLOTS), F32) if start else acc[g])
            if end:
                near_ref[g] = found.astype(BF)
            else:
                acc[g] = found
        found = choose(xhot, xlo, jnp.zeros((64, LANES), F32) if start else xacc[...])
        if end:
            extra_ref[0] = found.astype(BF)
        else:
            xacc[...] = found

    send_y(0)
    rim.start()
    for g in range(groups):
        lo, hi = coarse_slots(slots(nbr_ref, g, 0))
        los.append(lo)
        hots[g] = one_hot(hi)
    xlo, xhi = coarse_slots(clinks_ref[pl.ds(grp * (tiles // 4) + tile // 4, 1), :])
    xhot = one_hot(xhi)
    send_y(1)
    send_y(7)
    pick_own(2)
    send_y(2)
    send_y(6)
    pick_own(3)
    send_y(3)
    send_y(5)
    send_y(4)
    send_swap(0)
    for g in range(4, groups):
        pick_own(g)
    send_swap(1)
    send_swap(7)
    rim.wait()
    for g in range(groups):
        pick_rim(g)
    send_swap(2)
    send_swap(6)
    pick_coarse((0, 1), True, False)
    send_swap(3)
    send_swap(5)
    send_swap(4)
    pick_coarse((7, 2), False, False)
    pick_coarse((6, 3), False, False)
    pick_coarse((5, 4), False, True)
    own = held[z, y].reshape(64, WIDE)
    extra_ref[1] = jnp.where(grp == 1, own[:, LANES:].astype(F32), own[:, :LANES].astype(F32)).astype(BF)


def gather_call(coarse_shard, fine_probe, nbr, clinks):
    vmem = pl.BlockSpec(memory_space=pltpu.VMEM)
    dma = pltpu.SemaphoreType.DMA
    groups = nbr.shape[0] // GROUP
    near = jax.ShapeDtypeStruct((groups, 64, SLOTS), BF)
    return pl.pallas_call(
        gather_kernel,
        name="coarse_gather",
        out_shape=(near, near, jax.ShapeDtypeStruct((2, 64, LANES), BF)),
        in_specs=[vmem, pl.BlockSpec(memory_space=pl.ANY), vmem, vmem],
        out_specs=(vmem, vmem, vmem),
        scratch_shapes=[
            pltpu.VMEM((8, 64, LANES), BF),
            pltpu.VMEM((64, RIM + fine_probe.shape[1]), BF),
            pltpu.VMEM((8, 4, 2, 32, WIDE), BF),
            pltpu.VMEM((groups, WIDE, SLOTS), BF),
            pltpu.VMEM((groups, WIDE, SLOTS), BF),
            pltpu.VMEM((groups, 64, SLOTS), F32),
            pltpu.VMEM((64, LANES), F32),
            dma((7,)), dma((7,)), dma((7,)), dma((7,)), dma((8, 3)), dma((8, 3)), dma((8,)), dma((8,)),
            dma, dma, dma,
        ],
        compiler_params=pltpu.CompilerParams(
            collective_id=0, has_side_effects=True, vmem_limit_bytes=60 * 1024 * 1024
        ),
    )(coarse_shard, fine_probe, nbr, clinks)


def sum_kernel(
    terms_ref, fterms_ref, extra_ref, xown_ref, nbr_ref, clinks_ref, own_ref, back_ref, fine_ref, rim_in,
    hots, fhots, totals, rim_out, piece, half_out, half_in, acc, y_out, y_in, z_out, z_in, x_out, x_in,
    s1, r1, s2, r2, s3, r3, s4, r4, s5, r5, s6, s7,
):
    grp, z, y, x_hi, core = place()
    tile = lax.axis_index("tile")
    tiles = lax.axis_size("tile")
    right = (grp, (tile + 1) % tiles)
    left = (grp, (tile + tiles - 1) % tiles)
    mine = pl.ds(pl.multiple_of(core * 32, 32), 32)
    other = pl.ds(pl.multiple_of((1 - core) * 32, 32), 32)
    groups = nbr_ref.shape[0] // GROUP
    load = pltpu.make_async_copy(own_ref, totals, s6)
    load.start()
    barrier, count = greet(grp, z, y, x_hi, core, (left, right))
    los, flos = [], []
    for g in range(groups):
        lo, hi = coarse_slots(slots(nbr_ref, g, 0))
        los.append(lo.astype(BF))
        hots[g] = one_hot(hi)
    xlo, xhi = coarse_slots(clinks_ref[pl.ds(grp * (tiles // 4) + tile // 4, 1), :])
    xlo = xlo.astype(BF)
    xhot = one_hot(xhi)
    swap, along_y, along_z = {}, {}, {}

    def spread_coarse(pair):
        targets = [(z + dz) % 8 for dz in pair]

        def lay(terms, lo):
            zero = jnp.zeros_like(terms)
            return jnp.concatenate(
                [jnp.where(lo == (target * 4 + yy).astype(F32).astype(BF), terms, zero)
                 for target in targets for yy in range(4)],
                axis=0,
            )

        total = dot(lay(extra_ref[...], xlo), xhot, NT)
        for g in range(groups):
            total = total + dot(lay(terms_ref[g], los[g]), hots[g], NT)
        for j, dz in enumerate(pair):
            for yy in range(4):
                at = (j * 4 + yy) * 64
                part = total[at : at + 64]
                if dz == 0:
                    own, none = xown_ref[...], jnp.zeros((64, LANES), F32)
                    here = y == yy
                    part = part + jnp.concatenate(
                        [jnp.where(here & (grp == 0), own, none), jnp.where(here & (grp == 1), own, none)], axis=1
                    )
                piece[dz, yy] = part
                half_out[dz, yy] = piece[dz, yy, other, :].astype(BF)

    def send_swap(dz):
        swap[dz] = pltpu.make_async_remote_copy(
            src_ref=half_out.at[dz], dst_ref=half_in.at[dz], send_sem=s1.at[dz], recv_sem=r1.at[dz],
            device_id=dev(grp, z, y, x_hi, 1 - core), device_id_type=MESH,
        )
        swap[dz].start()

    def send_y(dz):
        swap[dz].wait()
        for yy in range(4):
            total = piece[dz, yy, mine, :] + half_in[dz, yy].astype(F32)
            acc[dz, yy] = total
            y_out[dz, yy] = total.astype(BF)
        for k in (1, 0, 2):
            copy = pltpu.make_async_remote_copy(
                src_ref=y_out.at[dz, (y + k + 1) % 4], dst_ref=y_in.at[dz, k],
                send_sem=s2.at[dz, k], recv_sem=r2.at[dz, k],
                device_id=dev(grp, z, (y + k + 1) % 4, x_hi, core), device_id_type=MESH,
            )
            copy.start()
            along_y[dz, k] = copy

    def send_z(dz):
        total = acc[dz, y]
        for k in range(3):
            along_y[dz, k].wait()
            total = total + y_in[dz, k].astype(F32)
        if dz == 0:
            return total
        z_out[dz - 1] = total.astype(BF)
        along_z[dz] = pltpu.make_async_remote_copy(
            src_ref=z_out.at[dz - 1], dst_ref=z_in.at[dz - 1], send_sem=s3.at[dz - 1], recv_sem=r3.at[dz - 1],
            device_id=dev(grp, (z + dz) % 8, y, x_hi, core), device_id_type=MESH,
        )
        along_z[dz].start()

    def spread_sum(first, parts, start):
        total = None
        for g in range(start, groups):
            found = dot(spread(fterms_ref[g], flos[g], first, parts), fhots[g], NT)
            total = found if total is None else total + found
        return total

    stores = []

    def spread_own(part):
        found = spread_sum(4 + part * PART, PART, part)
        for j in range(PART):
            at = (part * PART + j) * WIDE
            totals[:, at : at + WIDE] = totals[:, at : at + WIDE] + found[j * 64 : j * 64 + 64]
        at = pl.ds(part * PART * WIDE, PART * WIDE)
        store = pltpu.make_async_copy(totals.at[:, at], fine_ref.at[:, at], s7.at[part])
        store.start()
        stores.append(store)

    spread_coarse((4, 3))
    pl.semaphore_wait(barrier, count)
    send_swap(4)
    send_swap(3)
    spread_coarse((5, 2))
    send_swap(5)
    send_swap(2)
    send_y(4)
    send_y(3)
    spread_coarse((6, 1))
    send_swap(6)
    send_swap(1)
    send_y(5)
    send_y(2)
    spread_coarse((7, 0))
    send_swap(7)
    send_swap(0)
    send_y(6)
    send_y(1)
    send_z(4)
    send_z(3)
    for g in range(groups):
        lo, hi = fine_slots(nbr_ref, g)
        flos.append(lo.astype(BF))
        fhots[g] = one_hot(hi)
    send_y(7)
    send_y(0)
    send_z(5)
    send_z(2)
    rim_terms = spread_sum(0, 4, 0)
    for j in range(4):
        rim_out[:, j * WIDE : j * WIDE + WIDE] = rim_terms[j * 64 : j * 64 + 64].astype(BF)
    rim = pltpu.make_async_remote_copy(
        src_ref=rim_out, dst_ref=rim_in, send_sem=s5, recv_sem=r5,
        device_id=left, device_id_type=MESH,
    )
    rim.start()
    send_z(6)
    send_z(1)
    load.wait()
    send_z(7)
    total = send_z(0)
    spread_own(0)
    spread_own(1)
    for dz in (4, 3, 5, 2, 6, 1, 7):
        along_z[dz].wait()
        total = total + z_in[dz - 1].astype(F32)
    for g in range(2):
        x_out[g] = total[:, g * LANES : g * LANES + LANES]
    third = []
    spot = grp * 4 + x_hi * 2 + core
    for k, (g1, h1, c1) in enumerate(near_peers(grp, z, y, x_hi, core)):
        copy = pltpu.make_async_remote_copy(
            src_ref=x_out.at[g1], dst_ref=x_in.at[spot], send_sem=s4.at[k], recv_sem=r4.at[k],
            device_id=dev(g1, z, y, h1, c1), device_id_type=MESH,
        )
        copy.start()
        third.append(copy)
    x_in[spot] = x_out[grp]
    for part in range(2, groups):
        spread_own(part)
    rim.wait()
    for copy in third:
        copy.wait()
    which = x_hi * 2 + core
    total = jnp.concatenate(
        [(x_in[half] + x_in[2 + half]) + (x_in[4 + half] + x_in[6 + half]) for half in range(2)], axis=0
    ).T
    part = total[0:32]
    for k in range(1, 4):
        part = jnp.where(which == k, total[k * 32 : k * 32 + 32], part)
    back_ref[...] = part
    for store in stores:
        store.wait()


def sum_call(terms, fterms, xterms, xown, nbr, clinks, own_back):
    vmem = pl.BlockSpec(memory_space=pltpu.VMEM)
    away = pl.BlockSpec(memory_space=pl.ANY)
    dma = pltpu.SemaphoreType.DMA
    groups = nbr.shape[0] // GROUP
    return pl.pallas_call(
        sum_kernel,
        name="coarse_sum",
        out_shape=(
            jax.ShapeDtypeStruct((32, 64), F32),
            jax.ShapeDtypeStruct(own_back.shape, F32),
            jax.ShapeDtypeStruct((64, RIM), BF),
        ),
        in_specs=[vmem] * 6 + [away],
        out_specs=(vmem, away, vmem),
        scratch_shapes=[
            pltpu.VMEM((groups, WIDE, SLOTS), BF),
            pltpu.VMEM((groups, WIDE, SLOTS), BF),
            pltpu.VMEM(own_back.shape, F32),
            pltpu.VMEM((64, RIM), BF),
            pltpu.VMEM((8, 4, 64, WIDE), F32),
            pltpu.VMEM((8, 4, 32, WIDE), BF),
            pltpu.VMEM((8, 4, 32, WIDE), BF),
            pltpu.VMEM((8, 4, 32, WIDE), F32),
            pltpu.VMEM((8, 4, 32, WIDE), BF),
            pltpu.VMEM((8, 3, 32, WIDE), BF),
            pltpu.VMEM((7, 32, WIDE), BF),
            pltpu.VMEM((7, 32, WIDE), BF),
            pltpu.VMEM((2, 32, LANES), F32),
            pltpu.VMEM((8, 32, LANES), F32),
            dma((8,)), dma((8,)), dma((8, 3)), dma((8, 3)), dma((7,)), dma((7,)), dma((7,)), dma((7,)),
            dma, dma, dma, dma((groups,)),
        ],
        compiler_params=pltpu.CompilerParams(
            collective_id=1, has_side_effects=True, vmem_limit_bytes=60 * 1024 * 1024
        ),
    )(terms, fterms, xterms, xown, nbr, clinks, own_back)


def one_hot(hi):
    spots = lax.broadcasted_iota(jnp.int32, (WIDE, hi.shape[1]), 0)
    return jnp.where(spots == hi, jnp.float32(1), jnp.float32(0)).astype(BF)


def dot(a, b, dims):
    return lax.dot_general(a, b, dims, preferred_element_type=F32)


def picked(rows, hot, lo, first, acc):
    found = dot(rows, hot, NN)
    for j in range(found.shape[0] // 64):
        acc = jnp.where(lo == first + j, found[j * 64 : j * 64 + 64], acc)
    return acc


def spread(terms, lo, first, parts):
    zero = jnp.zeros_like(terms)
    return jnp.concatenate([jnp.where(lo == (first + j), terms, zero) for j in range(parts)], axis=0)


def halves(a, b):
    lane = lax.broadcasted_iota(jnp.int32, a.shape, 1)
    low = lane < 64
    return (
        jnp.where(low, a, pltpu.roll(b, 64, 1)),
        jnp.where(low, pltpu.roll(a, 64, 1), b),
    )


def lane_rows(ref, first, parts):
    return jnp.concatenate([ref[:, (first + j) * WIDE : (first + j + 1) * WIDE] for j in range(parts)], axis=0)


def slots(nbr_ref, g, which):
    rows = [nbr_ref[pl.ds(g * GROUP + r, 1), :] for r in range(GROUP)]
    return jnp.concatenate([halves(rows[r], rows[r + 1])[which] for r in range(0, GROUP, 2)], axis=1)


def fine_slots(nbr_ref, g):
    at = slots(nbr_ref, g, 1) - 8192
    return at >> 8, at & 255


def coarse_slots(at):
    lo = jnp.where(at < 0, -1, (at >> 7) & 31)
    return lo, ((at >> 12) << 7) + (at & 127)


def block_kernel(
    near_ref, fnear_ref, extra_ref, fine_ref, diag_ref, cond_ref, cdiag_ref, ccond_ref,
    out_ref, back_ref, cout_ref, terms_ref, fterms_ref, xterms_ref, xown_ref,
):
    g = pl.program_id(0)

    @pl.when(g == 0)
    def _():
        res = dot(cdiag_ref[...], extra_ref[1], NT) + dot(ccond_ref[...], extra_ref[0], NT)
        res = res.astype(BF)
        cout_ref[...] = res
        xown_ref[...] = dot(res, cdiag_ref[...], TN)
        xterms_ref[...] = dot(res, ccond_ref[...], TN).astype(BF)

    nears, results, backs = [], [], []
    for pair in range(GROUP // 2):
        lanes = slice(pair * LANES, pair * LANES + LANES)
        nears.extend(halves(near_ref[:, lanes].astype(F32), fnear_ref[:, lanes].astype(F32)))
    for r in range(GROUP):
        at = r * LANES
        both = jnp.concatenate([diag_ref[at : at + LANES, :], cond_ref[at : at + LANES, :]], axis=1)
        pair = jnp.concatenate([fine_ref[:, at : at + LANES], nears[r].astype(BF)], axis=1)
        results.append(dot(pair, both, NT).astype(BF))
    for r in range(GROUP):
        at = r * LANES
        out_ref[:, at : at + LANES] = results[r]
        both = jnp.concatenate([diag_ref[at : at + LANES, :], cond_ref[at : at + LANES, :]], axis=1)
        back = dot(results[r], both, NN)
        back_ref[:, at : at + LANES] = back[:, :LANES]
        backs.append(back[:, LANES:])
    terms = [halves(backs[r], backs[r + 1]) for r in range(0, GROUP, 2)]
    fterms_ref[...] = jnp.concatenate([pair[1] for pair in terms], axis=1).astype(BF)
    terms_ref[...] = jnp.concatenate([pair[0] for pair in terms], axis=1).astype(BF)


def block_call(near, fnear, extra, fine_probe, diag, cond, cdiag, ccond):
    pts = fine_probe.shape[1]
    steps = near.shape[0]
    whole = lambda *shape: pl.BlockSpec(shape, lambda g: (0,) * len(shape))
    span = GROUP * LANES
    columns = pl.BlockSpec((64, span), lambda g: (0, g))
    slotted = pl.BlockSpec((None, 64, SLOTS), lambda g: (g, 0, 0))
    rows = pl.BlockSpec((span, LANES), lambda g: (g, 0))
    return pl.pallas_call(
        block_kernel,
        name="blocks",
        grid=(steps,),
        out_shape=(
            jax.ShapeDtypeStruct((64, pts), BF),
            jax.ShapeDtypeStruct((64, pts), F32),
            jax.ShapeDtypeStruct((32, 64), BF),
            jax.ShapeDtypeStruct(near.shape, BF),
            jax.ShapeDtypeStruct(near.shape, BF),
            jax.ShapeDtypeStruct((64, LANES), BF),
            jax.ShapeDtypeStruct((64, LANES), F32),
        ),
        in_specs=[
            slotted, slotted, whole(2, 64, LANES), columns, rows, rows, whole(32, LANES), whole(32, LANES),
        ],
        out_specs=(
            columns, columns, whole(32, 64), slotted, slotted, whole(64, LANES), whole(64, LANES),
        ),
        compiler_params=pltpu.CompilerParams(vmem_limit_bytes=60 * 1024 * 1024),
    )(near, fnear, extra, fine_probe, diag, cond, cdiag, ccond)


def finish_kernel(fine_ref, rim_ref, out_ref, held, into, back):
    pts = fine_ref.shape[1]
    pieces = 10
    span = (pts - RIM) // (pieces - 1)
    spans = [pl.ds(k * span, span) for k in range(pieces - 1)] + [pl.ds(pts - RIM, RIM)]
    loads, stores = [], []
    for k, at in enumerate(spans):
        load = pltpu.make_async_copy(fine_ref.at[:, at], held.at[:, at], into.at[k])
        load.start()
        loads.append(load)
    for k, at in enumerate(spans):
        loads[k].wait()
        if k == pieces - 1:
            last = lax.axis_index("tile") == lax.axis_size("tile") - 1
            keep = jnp.where(last, jnp.float32(0), jnp.float32(1))
            held[:, pts - RIM :] = held[:, pts - RIM :] + rim_ref[...].astype(F32) * keep
        store = pltpu.make_async_copy(held.at[:, at], out_ref.at[:, at], back.at[k])
        store.start()
        stores.append(store)
    for store in stores:
        store.wait()


def finish_call(fine_back, rim):
    away = pl.BlockSpec(memory_space=pl.ANY)
    dma = pltpu.SemaphoreType.DMA
    return pl.pallas_call(
        finish_kernel,
        name="add_rim",
        out_shape=jax.ShapeDtypeStruct(fine_back.shape, F32),
        in_specs=[away, pl.BlockSpec(memory_space=pltpu.VMEM)],
        out_specs=away,
        scratch_shapes=[pltpu.VMEM(fine_back.shape, F32), dma((10,)), dma((10,))],
        compiler_params=pltpu.CompilerParams(vmem_limit_bytes=60 * 1024 * 1024),
    )(fine_back, rim)


def on_device(
    fine_probe, coarse_probe, fine_diag, fine_cond, fine_nbr, coarse_diag, coarse_cond, coarse_nbr
):
    near, fine_near, extra = gather_call(coarse_probe.T, fine_probe, fine_nbr, coarse_nbr)
    fine_out, own_back, coarse_out, terms, fine_terms, extra_terms, extra_own = block_call(
        near, fine_near, extra, fine_probe, fine_diag, fine_cond, coarse_diag, coarse_cond
    )
    coarse_back, fine_back, rim_in = sum_call(
        terms, fine_terms, extra_terms, extra_own, fine_nbr, coarse_nbr, own_back
    )
    fine_back = finish_call(fine_back, rim_in)
    return fine_out, fine_back, coarse_out.T, coarse_back.T


def solution(mesh):
    columns, rows = P(None, ("grp", "tile")), P(("grp", "tile"), None)
    return jax.shard_map(
        on_device,
        mesh=mesh,
        in_specs=(columns, columns, rows, rows, rows, rows, rows, P()),
        out_specs=(columns, columns, columns, columns),
        check_vma=False,
    )
```
